32 devices in a mesh: tile: 4 (over z), depth: 8 (over y, x, core).
Axes of the slice: x: 2, y: 2, z: 4, core: 2. Of those that a mesh axis runs over, the one named last changes fastest.
Arguments:
- velocity: float32 [3, 128, 96, 512], P(None, 'depth', None, 'tile'), may hold values from -6 to 6
- metric: float32 [96], replicated, may hold values from 0.5 to 2
- colour_map: bfloat16 [4, 128], replicated, may hold values from 0.049804688 to 1
- counts: int32 [96, 512], P(None, 'tile'), may hold values from 1 to 128
Outputs:
- rendered: float32 [4, 96, 512], P(None, 'depth', 'tile')
The draws below stay inside these ranges and needn't reach their ends.
Inputs may be any that keep to these rules, and one draw needn't show every extreme that they name: `counts`: each pixel's ray passes the cells with z below its count.
All inputs are finite; a program needn't handle non-finite values.
Results may differ from the reference program's by a relative error of at most 0.0003.
Values sent between devices are 32-bit elements; how exact they have to be, the bound alone decides.
No kernel may reach another device: no remote copies, remote signals or barrier semaphores. Data moves between devices by JAX's collectives and lax.ppermute only.
A program may use at most 64 MiB of HBM per device.

```python
import math
import jax
import jax.numpy as jnp
from jax import lax

CX = 128
NY = 96
NBINS = 128
NX = 512
NZ = 128
N_TILE = 4


def with_ends(drawn, key, low, top_value):
    longest = drawn.shape.index(max(drawn.shape))
    spots = []
    for shift in (0, 1):
        where = [jax.random.randint(jax.random.fold_in(key, axis), (), 0, length) for axis, length in enumerate(drawn.shape)]
        where[longest] = (where[longest] + shift) % drawn.shape[longest]
        spots.append(tuple(where))
    return drawn.at[spots[0]].set(low).at[spots[1]].set(top_value)


def level_of(rng, dims, pieces, smallest, largest):
    loudness, own = 1.0, jax.random.fold_in(rng, 6)
    for position, parts in pieces:
        steps = jnp.exp(jax.random.uniform(jax.random.fold_in(own, position), (parts,), jnp.float32, smallest / len(pieces), largest / len(pieces)))
        loudness = loudness * jnp.repeat(steps, dims[position] // parts).reshape([-1 if axis == position else 1 for axis in range(len(dims))])
    return loudness


def bell_draw(key, shape, deviation, bound, cuts=(), kind=jnp.bfloat16):
    gain = level_of(key, shape, cuts, -0.22, 0.18) if cuts else 1.0
    drawn = jax.random.normal(key, shape, jnp.float32) * deviation * gain
    return jnp.minimum(jnp.maximum(drawn, -bound), bound).astype(kind)


def setup_inputs(seed: int = 0) -> dict:
    streams_of = jax.random.split(jax.random.key(seed), 5)
    velocity = bell_draw(streams_of[0], (3, NZ, NY, NX), 1.0, 6.0, ((1, 8), (3, 4)), jnp.float32)
    metric = jnp.clip(jnp.exp(jax.random.uniform(streams_of[1], (NY,), jnp.float32, math.log(0.5), math.log(2.0))), 0.5, 2.0)
    colour_map = jnp.clip(jax.random.uniform(streams_of[2], (4, NBINS), jnp.float32, 0.049804688, 1.0), 0.049804688, 1.0).astype(jnp.bfloat16)
    counts = with_ends(jax.random.randint(streams_of[3], (NY, NX), 1, NZ + 1), jax.random.fold_in(streams_of[3], 1), 1, NZ).astype(jnp.int32)
    return {"velocity": velocity, "metric": metric, "colour_map": colour_map, "counts": counts}


STENCIL_WEIGHTS = (45.0 / 60.0, -9.0 / 60.0, 1.0 / 60.0)
CRITERION_SCALE = 2.0
VORTEX_SCALE = 4.0
OPTICAL_DEPTH = 4.0

def interior(padded, keep_dim):
    for dimension in range(3):
        if dimension != keep_dim:
            padded = lax.slice_in_dim(padded, 3, padded.shape[dimension] - 3, axis=dimension)
    return padded

def central(padded, dimension):
    extent = padded.shape[dimension] - 6
    result = None
    for offset, weight in zip((1, 2, 3), STENCIL_WEIGHTS):
        forward = lax.slice_in_dim(padded, 3 + offset, 3 + offset + extent, axis=dimension)
        backward = lax.slice_in_dim(padded, 3 - offset, 3 - offset + extent, axis=dimension)
        result = weight * (forward - backward) if result is None else result + weight * (forward - backward)
    return result

def gradients(padded, metric_rows):
    tensor = []
    for component in range(3):
        component_field = padded[component]
        stream_slope = central(interior(component_field, 2), 2)
        normal_slope = central(interior(component_field, 1), 1) * metric_rows[None, :, None]
        span_slope = central(interior(component_field, 0), 0)
        tensor.append((stream_slope, normal_slope, span_slope))
    return tensor

def invariants(tensor):
    contraction = jnp.zeros_like(tensor[0][0])
    for source in range(3):
        for target in range(3):
            contraction = contraction + tensor[source][target] * tensor[target][source]
    curl_first = tensor[2][1] - tensor[1][2]
    curl_second = tensor[0][2] - tensor[2][0]
    curl_third = tensor[1][0] - tensor[0][1]
    vortex = jnp.sqrt(curl_first * curl_first + curl_second * curl_second + curl_third * curl_third)
    return (-0.5 * contraction, vortex)

def reference(velocity, metric, colour_map, counts):
    map_float = colour_map.astype(jnp.float32)

    def render_block(block_start):
        columns = (block_start - 3 + jnp.arange(CX + 6, dtype=jnp.int32)) % NX
        section = jnp.take(velocity, columns, axis=3)
        section = jnp.pad(section, ((0, 0), (3, 3), (0, 0), (0, 0)), mode='wrap')
        section = jnp.pad(section, ((0, 0), (0, 0), (3, 3), (0, 0)))
        criterion, vortex = invariants(gradients(section, metric))
        bin_level = (NBINS - 1) * 0.5 * (1.0 + jnp.tanh(criterion / CRITERION_SCALE))
        lowbin = jnp.minimum(jnp.floor(bin_level), NBINS - 2).astype(jnp.int32)
        fraction = bin_level - lowbin.astype(bin_level.dtype)
        lower_value = jnp.take(map_float, lowbin, axis=1)
        upper_value = jnp.take(map_float, lowbin + 1, axis=1)
        values = (1.0 - fraction) * lower_value + fraction * upper_value
        count_block = lax.dynamic_slice_in_dim(counts, block_start, CX, 1)
        depth_index = jnp.arange(NZ, dtype=jnp.int32)[:, None, None]
        inside = depth_index < count_block[None]
        extinct = jnp.where(inside, values[0] * (OPTICAL_DEPTH / NZ), jnp.zeros_like(values[0]))
        opacity = -jnp.expm1(-extinct)
        emission = values[1:] * jnp.tanh(vortex / VORTEX_SCALE)[None]
        before = jnp.cumsum(extinct, axis=0) - extinct
        colour = lax.optimization_barrier(jnp.sum((jnp.exp(-before) * opacity)[None] * emission, axis=1))
        total = lax.optimization_barrier(jnp.sum(extinct, axis=0))
        return jnp.concatenate([colour, -jnp.expm1(-total)[None]], axis=0)
    block_starts = jnp.arange(N_TILE, dtype=jnp.int32) * CX
    stacked = lax.map(render_block, block_starts)
    return jnp.transpose(stacked, (1, 2, 0, 3)).reshape(4, NY, NX)
```

```python
import functools

import jax
import jax.numpy as jnp
from jax import lax
from jax.experimental import pallas as pl
from jax.experimental.pallas import tpu as pltpu
from jax.sharding import PartitionSpec as P

REACH = 3
SUB = 8
GROUP = 8
CRITERION_SCALE = 2.0
VORTEX_SCALE = 4.0
OPTICAL_DEPTH = 4.0
LOG2_E = 1.4426950408889634
TINY = 1.2e-38
MIB = 1024 * 1024
F32 = jnp.float32
BF16 = jnp.bfloat16


def parity():
    return lax.rem(lax.axis_index("depth"), 2)


def stencil(ahead, behind):
    return 45.0 * (ahead[0] - behind[0]) - 9.0 * (ahead[1] - behind[1]) + (ahead[2] - behind[2])


def weight_of(distance):
    out = jnp.zeros(distance.shape, F32)
    for k, weight in ((1, 45.0), (2, -9.0), (3, 1.0)):
        out = jnp.where(distance == k, weight, out)
        out = jnp.where(distance == -k, -weight, out)
    return out


def halves(x):
    high = x.astype(BF16)
    low = (x - high.astype(F32)).astype(BF16)
    return jnp.concatenate([high, low], axis=1)


def ends_kernel(vel, far, near, sems):
    slab = vel.shape[1]
    odd = parity()
    last = slab - REACH
    copies = [
        pltpu.make_async_copy(vel.at[:, pl.ds(odd * last, REACH)], far, sems.at[0]),
        pltpu.make_async_copy(vel.at[:, pl.ds((1 - odd) * last, REACH)], near, sems.at[1]),
    ]
    for copy in copies:
        copy.start()
    for copy in copies:
        copy.wait()


def edges_kernel(vel, right_out, left_out):
    slab, ny, cx = vel.shape[1:]
    half = ny // 2
    lane = lax.broadcasted_iota(jnp.int32, (SUB, cx), 1)

    def tile(t, _):
        for c in range(3):
            to_right = jnp.zeros((SUB, cx), F32)
            to_left = jnp.zeros((SUB, cx), F32)
            for z in range(slab):
                for h in range(2):
                    first = GROUP * z + 4 * h
                    rows = pl.ds(pl.multiple_of(h * half + t * SUB, SUB), SUB)
                    turned = pltpu.roll(vel[c, z, rows, :], (first + REACH) % cx, 1)
                    to_right = jnp.where((lane >= first) & (lane < first + 4), turned, to_right)
                    place = lax.rem(lane + (2 * cx - first - REACH), cx)
                    to_left = jnp.where(place < 4, turned, to_left)
            rows = pl.ds(pl.multiple_of(t * SUB, SUB), SUB)
            right_out[c, rows, :] = to_right
            left_out[c, rows, :] = to_left
        return 0

    lax.fori_loop(0, half // SUB, tile, 0)


def slopes_kernel(vel, near, metric, stream, span, outline, ext, band, sems):
    slab, ny, cx = vel.shape[1:]
    odd = parity()
    body = pl.ds(SUB, ny)
    copies = [
        pltpu.make_async_copy(vel, ext.at[:, pl.ds(REACH, slab), body, :], sems.at[0]),
        pltpu.make_async_copy(
            near, ext.at[:, pl.ds((1 - odd) * (slab + REACH), REACH), body, :], sems.at[1]),
    ]
    for copy in copies:
        copy.start()
    zero = jnp.zeros((SUB, cx), F32)
    blank = odd * (slab + REACH)
    for c in range(3):
        for z in range(slab):
            ext[c, REACH + z, pl.ds(0, SUB), :] = zero
            ext[c, REACH + z, pl.ds(ny + SUB, SUB), :] = zero
        for z in range(REACH):
            ext[c, blank + z, body, :] = jnp.zeros((ny, cx), F32)
    source = lax.broadcasted_iota(jnp.int32, (cx, cx), 0)
    target = lax.broadcasted_iota(jnp.int32, (cx, cx), 1)
    weights = weight_of(source - target).astype(BF16)
    band[pl.ds(0, cx), :] = weights
    band[pl.ds(cx, cx), :] = weights
    for copy in copies:
        copy.wait()

    def layer(z, _):
        rows = jnp.concatenate([halves(ext[c, REACH + z, body, :]) for c in range(3)], axis=0)
        along = jnp.dot(rows, band[...], preferred_element_type=F32)
        for c in range(3):
            stream[c, z] = along[c * ny : (c + 1) * ny]
        return 0

    lax.fori_loop(0, slab, layer, 0)
    row = lax.broadcasted_iota(jnp.int32, (SUB, cx), 0)

    def tile(t, _):
        base = pl.multiple_of(t * SUB, SUB)
        rows = pl.ds(base, SUB)
        inner = pl.ds(base + SUB, SUB)
        scale = jnp.zeros((SUB, cx), F32)
        for r in range(SUB):
            scale = jnp.where(row == r, metric[base + r], scale)

        def slopes(z):
            dy = [
                scale * stencil(
                    [ext[c, REACH + z, pl.ds(base + SUB + k, SUB), :] for k in (1, 2, 3)],
                    [ext[c, REACH + z, pl.ds(base + SUB - k, SUB), :] for k in (1, 2, 3)],
                )
                for c in range(3)
            ]
            dz = [
                stencil(
                    [ext[c, REACH + z + k, inner, :] for k in (1, 2, 3)],
                    [ext[c, REACH + z - k, inner, :] for k in (1, 2, 3)],
                )
                for c in range(3)
            ]
            return dy, dz

        for cell in range(slab - REACH):
            z = REACH * (1 - odd) + cell
            dy, dz = slopes(z)
            turn = dy[2] - dz[1]
            span[0, cell, rows, :] = dy[0]
            span[1, cell, rows, :] = dz[0]
            span[2, cell, rows, :] = dy[1] * dy[1] + dz[2] * dz[2] + 2.0 * (dy[2] * dz[1])
            span[3, cell, rows, :] = turn * turn
        for q in range(REACH):
            dy, dz = slopes(odd * (slab - 1 - 2 * q) + q)
            for c in range(3):
                outline[c, q, rows, :] = dy[c]
                outline[3 + c, q, rows, :] = dz[c]
        return 0

    lax.fori_loop(0, ny // SUB, tile, 0)


def tables(colour_map, total_depth):
    bins = colour_map.shape[1]
    table = colour_map[...].astype(F32)
    steps = pltpu.roll(table, bins - 1, 1) - table
    gain = -LOG2_E * OPTICAL_DEPTH / total_depth
    lower = [jnp.broadcast_to(table[k : k + 1], (SUB, bins)) for k in range(4)]
    rise = [jnp.broadcast_to(steps[k : k + 1], (SUB, bins)) for k in range(4)]
    lower[0] = lower[0] * gain
    rise[0] = rise[0] * gain
    return lower, rise


def shade(square, spin, seen, lower, rise):
    bins = lower[0].shape[1]
    half_top = (bins - 1) * 0.5
    level = half_top + half_top * jnp.tanh(square * (-0.5 / (3600.0 * CRITERION_SCALE)))
    low = jnp.minimum(jnp.floor(level), bins - 2.0)
    fraction = level - low
    index = low.astype(jnp.int32)

    def value(k):
        first = jnp.take_along_axis(lower[k], index, axis=1)
        return first + fraction * jnp.take_along_axis(rise[k], index, axis=1)

    passed = jnp.exp2(jnp.where(seen, value(0), 0.0))
    length = spin * lax.rsqrt(jnp.maximum(spin, TINY))
    strength = jnp.tanh(length * (1.0 / (60.0 * VORTEX_SCALE)))
    return passed, [value(k) for k in (1, 2, 3)], strength


def inner_kernel(
    total_depth, stream, span, from_left, from_right, counts, colour_map,
    part, stream_out, along, packed, place,
):
    slab, ny, cx = stream.shape[1:]
    half = ny // 2
    odd = parity()
    lane = lax.broadcasted_iota(jnp.int32, (SUB, cx), 1)
    within = lax.rem(lane, GROUP)

    def pack(t, _):
        rows = pl.ds(pl.multiple_of(2 * t * SUB, 2 * SUB), 2 * SUB)
        wide = lax.rem(lax.broadcasted_iota(jnp.int32, (2 * SUB, cx), 1), GROUP)
        for c in range(3):
            right = from_left[c, rows, :]
            left = from_right[c, rows, :]
            first = jnp.where(wide < 3, right, left)
            second = pltpu.roll(jnp.where((wide >= 4) & (wide < 7), right, left), cx - 4, 1)
            at = pl.multiple_of(c * ny + 2 * t * SUB, 2 * SUB)
            packed[pl.ds(at, 2 * SUB), :] = halves(first)
            packed[pl.ds(pl.multiple_of(at + half, 2 * SUB), 2 * SUB), :] = halves(second)
        return 0

    lax.fori_loop(0, half // (2 * SUB), pack, 0)
    place[...] = jnp.zeros(place.shape, F32)
    source = lax.broadcasted_iota(jnp.int32, (SUB, cx), 0)
    column = jnp.where(source < REACH, source - REACH, source - REACH + cx)
    weights = weight_of(column - lane)
    place[pl.ds(cx, SUB), :] = jnp.where(source < 2 * REACH, weights, 0.0)

    def layer(z, _):
        spread = place[pl.ds(pl.multiple_of(cx - GROUP * z, SUB), cx), :].astype(BF16)
        add = jnp.dot(
            packed[...], jnp.concatenate([spread, spread], axis=0), preferred_element_type=F32
        )
        for c in range(3):
            along[c, z] = stream[c, z] + add[c * ny : (c + 1) * ny]
        return 0

    lax.fori_loop(0, slab, layer, 0)
    for q in range(REACH):
        z = odd * (slab - 1 - 2 * q) + q
        for c in range(3):
            stream_out[c, q] = along[c, z]

    lower, rise = tables(colour_map, total_depth)
    start = REACH * (1 - odd)
    first_depth = lax.axis_index("depth") * slab + start

    def tile(t, _):
        rows = pl.ds(pl.multiple_of(t * SUB, SUB), SUB)
        count = counts[rows, :] - first_depth
        colour = [jnp.zeros((SUB, cx), F32) for _ in range(3)]
        clear = jnp.ones((SUB, cx), F32)
        for cell in range(slab - REACH):
            dx = [along[c, start + cell, rows, :] for c in range(3)]
            dy, dz, rest, turn = [span[k, cell, rows, :] for k in range(4)]
            square = rest + dx[0] * dx[0] + 2.0 * (dy * dx[1] + dz * dx[2])
            w1 = dz - dx[2]
            w2 = dx[1] - dy
            spin = turn + w1 * w1 + w2 * w2
            passed, values, strength = shade(square, spin, count > cell, lower, rise)
            after = clear * passed
            weight = (clear - after) * strength
            colour = [colour[k] + weight * values[k] for k in range(3)]
            clear = after
        for k in range(3):
            part[k, rows, :] = colour[k]
        part[3, rows, :] = clear
        return 0

    lax.fori_loop(0, ny // SUB, tile, 0)


def outer_kernel(total_depth, far, outline, stream, part, counts, colour_map, out, whole):
    ny, cx = counts.shape
    odd = parity()
    lower, rise = tables(colour_map, total_depth)
    slab = total_depth // lax.axis_size("depth")
    slab_first = lax.axis_index("depth") * slab
    sign = jnp.full((SUB, cx), 2 * odd - 1, jnp.int32).astype(F32)
    front = jnp.full((SUB, cx), odd, jnp.int32) == 0
    weights = [45.0 * sign, -9.0 * sign, sign]

    def tile(t, _):
        rows = pl.ds(pl.multiple_of(t * SUB, SUB), SUB)
        count = counts[rows, :] - slab_first
        beyond = [
            [far[c, (1 - odd) * (2 - 2 * r) + r, rows, :] for r in range(REACH)] for c in range(3)
        ]
        layers = []
        for q in range(REACH):
            dx = [stream[c, q, rows, :] for c in range(3)]
            dy = [outline[c, q, rows, :] for c in range(3)]
            dz = [outline[3 + c, q, rows, :] for c in range(3)]
            for c in range(3):
                for r in range(REACH - q):
                    dz[c] = dz[c] + weights[q + r] * beyond[c][r]
            w0 = dy[2] - dz[1]
            w1 = dz[0] - dx[2]
            w2 = dx[1] - dy[0]
            square = dx[0] * dx[0] + dy[1] * dy[1] + dz[2] * dz[2]
            square = square + 2.0 * (dy[0] * dx[1] + dz[0] * dx[2] + dz[1] * dy[2])
            spin = w0 * w0 + w1 * w1 + w2 * w2
            seen = count > odd * (slab - 1 - 2 * q) + q
            passed, values, strength = shade(square, spin, seen, lower, rise)
            weight = (1.0 - passed) * strength
            layers.append([weight * value for value in values] + [passed])
        first = [jnp.where(front, a, b) for a, b in zip(layers[0], layers[2])]
        last = [jnp.where(front, b, a) for a, b in zip(layers[0], layers[2])]
        clear = first[3] * layers[1][3]
        rest = part[3, rows, :]
        outer_clear = clear * last[3]
        for k in range(3):
            own = first[k] + first[3] * layers[1][k] + clear * last[k]
            inner = part[k, rows, :]
            whole[k, rows, :] = jnp.where(front, own + outer_clear * inner, inner + rest * own)
        whole[3, rows, :] = outer_clear * rest
        return 0

    lax.fori_loop(0, ny // SUB, tile, 0)
    share = out.shape[1] // 4
    for j in range(out.shape[0]):
        for k in range(4):
            out[j, pl.ds(k * share, share), :] = whole[k, pl.ds(j * share, share), :]


def join_kernel(parts, out):
    share = out.shape[0]

    def channel(j, k):
        return parts[j, pl.ds(k * share, share), :]

    colour = [channel(0, k) for k in range(3)]
    clear = channel(0, 3)
    for j in range(1, parts.shape[0]):
        colour = [colour[k] + clear * channel(j, k) for k in range(3)]
        clear = clear * channel(j, 3)
    for k in range(3):
        out[:, k, :] = colour[k]
    out[:, 3, :] = 1.0 - clear


def vmem(count):
    return [pl.BlockSpec(memory_space=pltpu.VMEM)] * count


def shape(*dims):
    return jax.ShapeDtypeStruct(dims, F32)


def per_device(velocity, metric, colour_map, counts):
    _, slab, ny, cx = velocity.shape
    devices = lax.axis_size("depth")
    tiles = lax.axis_size("tile")
    total_depth = slab * devices
    hbm = pl.BlockSpec(memory_space=pltpu.HBM)
    scalars = pl.BlockSpec(memory_space=pltpu.SMEM)
    inner_layers = slab - REACH

    def limit(size):
        return pltpu.CompilerParams(vmem_limit_bytes=size * MIB)

    far, near = pl.pallas_call(
        ends_kernel,
        out_shape=(shape(3, REACH, ny, cx), shape(3, REACH, ny, cx)),
        in_specs=[hbm],
        out_specs=tuple(vmem(2)),
        scratch_shapes=[pltpu.SemaphoreType.DMA((2,))],
        compiler_params=limit(4),
        name="ends",
    )(velocity)
    up = [(i, (i + 1) % devices) for i in range(devices)]
    down = [(i, (i - 1) % devices) for i in range(devices)]
    far = lax.ppermute(far, "depth", [(up if i % 2 else down)[i] for i in range(devices)])
    near = lax.ppermute(near, "depth", [(down if i % 2 else up)[i] for i in range(devices)])

    own_right, own_left = pl.pallas_call(
        edges_kernel,
        out_shape=(shape(3, ny // 2, cx), shape(3, ny // 2, cx)),
        in_specs=vmem(1),
        out_specs=tuple(vmem(2)),
        compiler_params=limit(8),
        name="edges",
    )(velocity)
    from_left = lax.ppermute(own_right, "tile", [(i, (i + 1) % tiles) for i in range(tiles)])
    from_right = lax.ppermute(own_left, "tile", [(i, (i - 1) % tiles) for i in range(tiles)])

    stream, span, outline = pl.pallas_call(
        slopes_kernel,
        out_shape=(
            shape(3, slab, ny, cx),
            shape(4, inner_layers, ny, cx),
            shape(6, REACH, ny, cx),
        ),
        in_specs=[hbm] + vmem(1) + [scalars],
        out_specs=tuple(vmem(3)),
        scratch_shapes=[
            pltpu.VMEM((3, slab + 2 * REACH, ny + 2 * SUB, cx), F32),
            pltpu.VMEM((2 * cx, cx), BF16),
            pltpu.SemaphoreType.DMA((2,)),
        ],
        compiler_params=limit(16),
        cost_estimate=pl.CostEstimate(flops=10**9, bytes_accessed=10**7, transcendentals=0),
        name="slopes",
    )(velocity, near, metric)

    part, stream = pl.pallas_call(
        functools.partial(inner_kernel, total_depth),
        out_shape=(shape(4, ny, cx), shape(3, REACH, ny, cx)),
        in_specs=vmem(6),
        out_specs=tuple(vmem(2)),
        scratch_shapes=[
            pltpu.VMEM((3, slab, ny, cx), F32),
            pltpu.VMEM((3 * ny, 2 * cx), BF16),
            pltpu.VMEM((2 * cx, cx), F32),
        ],
        compiler_params=limit(16),
        cost_estimate=pl.CostEstimate(flops=10**9, bytes_accessed=10**7, transcendentals=0),
        name="inner",
    )(stream, span, from_left, from_right, counts, colour_map)

    parts = pl.pallas_call(
        functools.partial(outer_kernel, total_depth),
        out_shape=shape(devices, 4 * (ny // devices), cx),
        in_specs=vmem(6),
        out_specs=vmem(1)[0],
        scratch_shapes=[pltpu.VMEM((4, ny, cx), F32)],
        compiler_params=limit(16),
        name="outer",
    )(far, outline, stream, part, counts, colour_map)
    parts = lax.all_to_all(parts, "depth", 0, 0, tiled=True)
    image = pl.pallas_call(
        join_kernel,
        out_shape=shape(ny // devices, 4, cx),
        in_specs=vmem(1),
        out_specs=vmem(1)[0],
        name="join",
    )(parts)
    return jnp.transpose(image, (1, 0, 2))


def solution(mesh):
    in_specs = (P(None, "depth", None, "tile"), P(), P(), P(None, "tile"))
    out_specs = P(None, "depth", "tile")
    return jax.shard_map(
        per_device, mesh=mesh, in_specs=in_specs, out_specs=out_specs, check_vma=False
    )
```

```python
import functools
import math

import jax
import jax.numpy as jnp
from jax import lax
from jax.experimental import pallas as pl
from jax.experimental.pallas import tpu as pltpu
from jax.sharding import PartitionSpec as P

REACH = 3
SUB = 8
GROUP = 8
CRITERION_SCALE = 2.0
VORTEX_SCALE = 4.0
OPTICAL_DEPTH = 4.0
LOG2_E = 1.4426950408889634
TINY = 1.2e-38
FIELD = 13
UNIT = 4096.0
MIB = 1024 * 1024
F32 = jnp.float32
BF16 = jnp.bfloat16


def parity():
    return lax.rem(lax.axis_index("depth"), 2)


def stencil(ahead, behind):
    return 45.0 * (ahead[0] - behind[0]) - 9.0 * (ahead[1] - behind[1]) + (ahead[2] - behind[2])


def weight_of(distance):
    out = jnp.zeros(distance.shape, F32)
    for k, weight in ((1, 45.0), (2, -9.0), (3, 1.0)):
        out = jnp.where(distance == k, weight, out)
        out = jnp.where(distance == -k, -weight, out)
    return out


def halves(x):
    high = x.astype(BF16)
    low = (x - high.astype(F32)).astype(BF16)
    return jnp.concatenate([high, low], axis=1)


def ends_kernel(vel, far, near, sems):
    odd = parity()
    last = vel.shape[1] - REACH
    copies = [
        pltpu.make_async_copy(vel.at[:, pl.ds(odd * last, REACH)], far, sems.at[0]),
        pltpu.make_async_copy(vel.at[:, pl.ds((1 - odd) * last, REACH)], near, sems.at[1]),
    ]
    for copy in copies:
        copy.start()
    for copy in copies:
        copy.wait()


def edges_kernel(vel, ext, right_out, left_out, sem):
    slab, ny, cx = vel.shape[1:]
    half = ny // 2
    body = pl.ds(SUB, ny)
    copy = pltpu.make_async_copy(vel, ext.at[:, pl.ds(REACH, slab), body, :], sem.at[0])
    copy.start()
    zero = jnp.zeros((SUB, cx), F32)
    for c in range(3):
        for z in range(slab):
            ext[c, REACH + z, pl.ds(0, SUB), :] = zero
            ext[c, REACH + z, pl.ds(ny + SUB, SUB), :] = zero
    lane = lax.broadcasted_iota(jnp.int32, (SUB, cx), 1)

    def tile(t, _):
        for c in range(3):
            to_right = jnp.zeros((SUB, cx), F32)
            to_left = jnp.zeros((SUB, cx), F32)
            for z in range(slab):
                for h in range(2):
                    first = GROUP * z + 4 * h
                    rows = pl.ds(pl.multiple_of(h * half + t * SUB, SUB), SUB)
                    turned = pltpu.roll(vel[c, z, rows, :], (first + REACH) % cx, 1)
                    to_right = jnp.where((lane >= first) & (lane < first + 4), turned, to_right)
                    place = lax.rem(lane + (2 * cx - first - REACH), cx)
                    to_left = jnp.where(place < 4, turned, to_left)
            rows = pl.ds(pl.multiple_of(t * SUB, SUB), SUB)
            right_out[c, rows, :] = to_right
            left_out[c, rows, :] = to_left
        return 0

    lax.fori_loop(0, half // SUB, tile, 0)
    copy.wait()


def slopes_kernel(ext_in, near, metric, stream, span, outline, ext, band):
    del ext_in
    slab, ny, cx = stream.shape[1:]
    odd = parity()
    body = pl.ds(SUB, ny)
    known = (1 - odd) * (slab + REACH)
    blank = odd * (slab + REACH)
    for c in range(3):
        for z in range(REACH):
            ext[c, known + z, body, :] = near[c, z]
            ext[c, blank + z, body, :] = jnp.zeros((ny, cx), F32)
    source = lax.broadcasted_iota(jnp.int32, (cx, cx), 0)
    target = lax.broadcasted_iota(jnp.int32, (cx, cx), 1)
    weights = weight_of(source - target).astype(BF16)
    band[pl.ds(0, cx), :] = weights
    band[pl.ds(cx, cx), :] = weights
    row = lax.broadcasted_iota(jnp.int32, (SUB, cx), 0)
    steps = math.gcd(slab, ny // SUB)
    layers = slab // steps
    tiles = ny // SUB // steps

    def along(z):
        rows = jnp.concatenate([halves(ext[c, REACH + z, body, :]) for c in range(3)], axis=0)
        out = jnp.dot(rows, band[...], preferred_element_type=F32)
        for c in range(3):
            stream[c, z] = out[c * ny : (c + 1) * ny]

    def tile(t):
        base = pl.multiple_of(t * SUB, SUB)
        rows = pl.ds(base, SUB)
        inner = pl.ds(base + SUB, SUB)
        scale = jnp.zeros((SUB, cx), F32)
        for r in range(SUB):
            scale = jnp.where(row == r, metric[base + r], scale)

        def slopes(z):
            dy = [
                scale * stencil(
                    [ext[c, REACH + z, pl.ds(base + SUB + k, SUB), :] for k in (1, 2, 3)],
                    [ext[c, REACH + z, pl.ds(base + SUB - k, SUB), :] for k in (1, 2, 3)],
                )
                for c in range(3)
            ]
            dz = [
                stencil(
                    [ext[c, REACH + z + k, inner, :] for k in (1, 2, 3)],
                    [ext[c, REACH + z - k, inner, :] for k in (1, 2, 3)],
                )
                for c in range(3)
            ]
            return dy, dz

        for cell in range(slab - REACH):
            z = REACH * (1 - odd) + cell
            dy, dz = slopes(z)
            turn = dy[2] - dz[1]
            span[0, cell, rows, :] = dy[0]
            span[1, cell, rows, :] = dz[0]
            span[2, cell, rows, :] = dy[1] * dy[1] + dz[2] * dz[2] + 2.0 * (dy[2] * dz[1])
            span[3, cell, rows, :] = turn * turn
        for q in range(REACH):
            dy, dz = slopes(odd * (slab - 1 - 2 * q) + q)
            for c in range(3):
                outline[c, q, rows, :] = dy[c]
                outline[3 + c, q, rows, :] = dz[c]

    def step(s, _):
        for k in range(layers):
            along(s * layers + k)
        for k in range(tiles):
            tile(s * tiles + k)
        return 0

    lax.fori_loop(0, steps, step, 0)


def tables(colour_map):
    bins = colour_map.shape[1]
    table = colour_map[...].astype(F32) * UNIT
    after = pltpu.roll(table, bins - 1, 1)
    packed = table.astype(jnp.int32) * (1 << FIELD) + after.astype(jnp.int32)
    return [jnp.broadcast_to(packed[k : k + 1], (SUB, bins)) for k in range(4)]


def shade(square, spin, seen, pairs, total_depth):
    bins = pairs[0].shape[1]
    half_top = (bins - 1) * 0.5
    level = half_top + half_top * jnp.tanh(square * (-0.5 / (3600.0 * CRITERION_SCALE)))
    low = jnp.minimum(jnp.floor(level), bins - 2.0)
    fraction = level - low
    index = low.astype(jnp.int32)

    def value(k):
        pair = jnp.take_along_axis(pairs[k], index, axis=1)
        first = lax.shift_right_logical(pair, FIELD).astype(F32)
        second = (pair & ((1 << FIELD) - 1)).astype(F32)
        return first + fraction * (second - first)

    gain = -LOG2_E * OPTICAL_DEPTH / (total_depth * UNIT)
    passed = jnp.exp2(jnp.where(seen, value(0) * gain, 0.0))
    length = spin * lax.rsqrt(jnp.maximum(spin, TINY))
    strength = jnp.tanh(length * (1.0 / (60.0 * VORTEX_SCALE)))
    return passed, [value(k) for k in (1, 2, 3)], strength


def inner_kernel(
    total_depth, stream, span, from_left, from_right, counts, colour_map,
    part, stream_out, along, packed, place,
):
    slab, ny, cx = stream.shape[1:]
    half = ny // 2
    odd = parity()
    lane = lax.broadcasted_iota(jnp.int32, (SUB, cx), 1)
    within = lax.rem(lane, GROUP)

    def pack(t, _):
        rows = pl.ds(pl.multiple_of(2 * t * SUB, 2 * SUB), 2 * SUB)
        wide = lax.rem(lax.broadcasted_iota(jnp.int32, (2 * SUB, cx), 1), GROUP)
        for c in range(3):
            right = from_left[c, rows, :]
            left = from_right[c, rows, :]
            first = jnp.where(wide < 3, right, left)
            second = pltpu.roll(jnp.where((wide >= 4) & (wide < 7), right, left), cx - 4, 1)
            at = pl.multiple_of(c * ny + 2 * t * SUB, 2 * SUB)
            packed[pl.ds(at, 2 * SUB), :] = halves(first)
            packed[pl.ds(pl.multiple_of(at + half, 2 * SUB), 2 * SUB), :] = halves(second)
        return 0

    lax.fori_loop(0, half // (2 * SUB), pack, 0)
    place[...] = jnp.zeros(place.shape, F32)
    source = lax.broadcasted_iota(jnp.int32, (SUB, cx), 0)
    column = jnp.where(source < REACH, source - REACH, source - REACH + cx)
    weights = weight_of(column - lane)
    place[pl.ds(cx, SUB), :] = jnp.where(source < 2 * REACH, weights, 0.0)

    together = math.gcd(slab, 4)

    def layers(s, _):
        spread = jnp.concatenate(
            [
                place[pl.ds(pl.multiple_of(cx - GROUP * (s * together + k), SUB), cx), :].astype(BF16)
                for k in range(together)
            ],
            axis=1,
        )
        add = jnp.dot(
            packed[...], jnp.concatenate([spread, spread], axis=0), preferred_element_type=F32
        )
        for k in range(together):
            z = s * together + k
            for c in range(3):
                along[c, z] = stream[c, z] + add[c * ny : (c + 1) * ny, k * cx : (k + 1) * cx]
        return 0

    lax.fori_loop(0, slab // together, layers, 0)
    for q in range(REACH):
        z = odd * (slab - 1 - 2 * q) + q
        for c in range(3):
            stream_out[c, q] = along[c, z]

    pairs = tables(colour_map)
    start = REACH * (1 - odd)
    first_depth = lax.axis_index("depth") * slab + start

    def tile(t, _):
        rows = pl.ds(pl.multiple_of(t * SUB, SUB), SUB)
        count = counts[rows, :] - first_depth
        colour = [jnp.zeros((SUB, cx), F32) for _ in range(3)]
        clear = jnp.ones((SUB, cx), F32)
        for cell in range(slab - REACH):
            dx = [along[c, start + cell, rows, :] for c in range(3)]
            dy, dz, rest, turn = [span[k, cell, rows, :] for k in range(4)]
            square = rest + dx[0] * dx[0] + 2.0 * (dy * dx[1] + dz * dx[2])
            w1 = dz - dx[2]
            w2 = dx[1] - dy
            spin = turn + w1 * w1 + w2 * w2
            passed, values, strength = shade(square, spin, count > cell, pairs, total_depth)
            after = clear * passed
            weight = (clear - after) * strength
            colour = [colour[k] + weight * values[k] for k in range(3)]
            clear = after
        for k in range(3):
            part[k, rows, :] = colour[k] * (1.0 / UNIT)
        part[3, rows, :] = clear
        return 0

    lax.fori_loop(0, ny // SUB, tile, 0)


def outer_kernel(total_depth, far, outline, stream, part, counts, colour_map, out, whole):
    ny, cx = counts.shape
    odd = parity()
    pairs = tables(colour_map)
    slab = total_depth // lax.axis_size("depth")
    slab_first = lax.axis_index("depth") * slab
    sign = jnp.full((SUB, cx), 2 * odd - 1, jnp.int32).astype(F32)
    front = jnp.full((SUB, cx), odd, jnp.int32) == 0
    weights = [45.0 * sign, -9.0 * sign, sign]

    def tile(t, _):
        rows = pl.ds(pl.multiple_of(t * SUB, SUB), SUB)
        count = counts[rows, :] - slab_first
        beyond = [
            [far[c, (1 - odd) * (2 - 2 * r) + r, rows, :] for r in range(REACH)] for c in range(3)
        ]
        layers = []
        for q in range(REACH):
            dx = [stream[c, q, rows, :] for c in range(3)]
            dy = [outline[c, q, rows, :] for c in range(3)]
            dz = [outline[3 + c, q, rows, :] for c in range(3)]
            for c in range(3):
                for r in range(REACH - q):
                    dz[c] = dz[c] + weights[q + r] * beyond[c][r]
            w0 = dy[2] - dz[1]
            w1 = dz[0] - dx[2]
            w2 = dx[1] - dy[0]
            square = dx[0] * dx[0] + dy[1] * dy[1] + dz[2] * dz[2]
            square = square + 2.0 * (dy[0] * dx[1] + dz[0] * dx[2] + dz[1] * dy[2])
            spin = w0 * w0 + w1 * w1 + w2 * w2
            seen = count > odd * (slab - 1 - 2 * q) + q
            passed, values, strength = shade(square, spin, seen, pairs, total_depth)
            weight = (1.0 - passed) * (strength * (1.0 / UNIT))
            layers.append([weight * value for value in values] + [passed])
        first = [jnp.where(front, a, b) for a, b in zip(layers[0], layers[2])]
        last = [jnp.where(front, b, a) for a, b in zip(layers[0], layers[2])]
        clear = first[3] * layers[1][3]
        rest = part[3, rows, :]
        outer_clear = clear * last[3]
        for k in range(3):
            own = first[k] + first[3] * layers[1][k] + clear * last[k]
            inner = part[k, rows, :]
            whole[k, rows, :] = jnp.where(front, own + outer_clear * inner, inner + rest * own)
        whole[3, rows, :] = outer_clear * rest
        return 0

    lax.fori_loop(0, ny // SUB, tile, 0)
    share = out.shape[1] // 4
    for j in range(out.shape[0]):
        for k in range(4):
            out[j, pl.ds(k * share, share), :] = whole[k, pl.ds(j * share, share), :]


def join_kernel(parts, out):
    share = out.shape[0]

    def channel(j, k):
        return parts[j, pl.ds(k * share, share), :]

    colour = [channel(0, k) for k in range(3)]
    clear = channel(0, 3)
    for j in range(1, parts.shape[0]):
        colour = [colour[k] + clear * channel(j, k) for k in range(3)]
        clear = clear * channel(j, 3)
    for k in range(3):
        out[:, k, :] = colour[k]
    out[:, 3, :] = 1.0 - clear


def vmem(count):
    return [pl.BlockSpec(memory_space=pltpu.VMEM)] * count


def shape(*dims):
    return jax.ShapeDtypeStruct(dims, F32)


def per_device(velocity, metric, colour_map, counts):
    _, slab, ny, cx = velocity.shape
    devices = lax.axis_size("depth")
    tiles = lax.axis_size("tile")
    total_depth = slab * devices
    scalars = pl.BlockSpec(memory_space=pltpu.SMEM)
    inner_layers = slab - REACH

    def limit(size):
        return pltpu.CompilerParams(vmem_limit_bytes=size * MIB)

    hbm = pl.BlockSpec(memory_space=pltpu.HBM)
    ends = (3, REACH, ny, cx)
    padded = (3, slab + 2 * REACH, ny + 2 * SUB, cx)
    columns = (3, ny // 2, cx)
    up = [(i, (i + 1) % devices) for i in range(devices)]
    down = [(i, (i - 1) % devices) for i in range(devices)]
    whole = pltpu.with_memory_space_constraint(velocity, pltpu.HBM)
    far, near = pl.pallas_call(
        ends_kernel,
        out_shape=(pltpu.VMEM(ends, F32), pltpu.VMEM(ends, F32)),
        in_specs=[hbm],
        out_specs=tuple(vmem(2)),
        scratch_shapes=[pltpu.SemaphoreType.DMA((2,))],
        compiler_params=limit(4),
        name="ends",
    )(whole)
    near = lax.ppermute(near, "depth", [(down if i % 2 else up)[i] for i in range(devices)])
    far = lax.ppermute(far, "depth", [(up if i % 2 else down)[i] for i in range(devices)])

    ext, to_right, to_left = pl.pallas_call(
        edges_kernel,
        out_shape=(pltpu.VMEM(padded, F32), pltpu.VMEM(columns, F32), pltpu.VMEM(columns, F32)),
        in_specs=vmem(1),
        out_specs=tuple(vmem(3)),
        scratch_shapes=[pltpu.SemaphoreType.DMA((1,))],
        compiler_params=limit(4),
        name="edges",
    )(velocity)
    from_left = lax.ppermute(to_right, "tile", [(i, (i + 1) % tiles) for i in range(tiles)])
    from_right = lax.ppermute(to_left, "tile", [(i, (i - 1) % tiles) for i in range(tiles)])

    stream, span, outline, _ = pl.pallas_call(
        slopes_kernel,
        out_shape=(
            shape(3, slab, ny, cx),
            shape(4, inner_layers, ny, cx),
            shape(6, REACH, ny, cx),
            shape(*padded),
        ),
        in_specs=vmem(2) + [scalars],
        out_specs=tuple(vmem(4)),
        scratch_shapes=[pltpu.VMEM((2 * cx, cx), BF16)],
        input_output_aliases={0: 3},
        compiler_params=limit(16),
        name="slopes",
    )(ext, near, metric)

    part, stream = pl.pallas_call(
        functools.partial(inner_kernel, total_depth),
        out_shape=(shape(4, ny, cx), shape(3, REACH, ny, cx)),
        in_specs=vmem(6),
        out_specs=tuple(vmem(2)),
        scratch_shapes=[
            pltpu.VMEM((3, slab, ny, cx), F32),
            pltpu.VMEM((3 * ny, 2 * cx), BF16),
            pltpu.VMEM((2 * cx, cx), F32),
        ],
        compiler_params=limit(16),
        name="inner",
    )(stream, span, from_left, from_right, counts, colour_map)

    parts = pl.pallas_call(
        functools.partial(outer_kernel, total_depth),
        out_shape=shape(devices, 4 * (ny // devices), cx),
        in_specs=vmem(6),
        out_specs=vmem(1)[0],
        scratch_shapes=[pltpu.VMEM((4, ny, cx), F32)],
        compiler_params=limit(16),
        name="outer",
    )(far, outline, stream, part, counts, colour_map)
    parts = lax.all_to_all(parts, "depth", 0, 0, tiled=True)
    image = pl.pallas_call(
        join_kernel,
        out_shape=shape(ny // devices, 4, cx),
        in_specs=vmem(1),
        out_specs=vmem(1)[0],
        name="join",
    )(parts)
    return jnp.transpose(image, (1, 0, 2))


def solution(mesh):
    in_specs = (P(None, "depth", None, "tile"), P(), P(), P(None, "tile"))
    out_specs = P(None, "depth", "tile")
    return jax.shard_map(
        per_device, mesh=mesh, in_specs=in_specs, out_specs=out_specs, check_vma=False
    )
```

```python
import functools
import math

import jax
import jax.numpy as jnp
from jax import lax
from jax.experimental import pallas as pl
from jax.experimental.pallas import tpu as pltpu
from jax.sharding import PartitionSpec as P

REACH = 3
SUB = 8
GROUP = 8
CRITERION_SCALE = 2.0
VORTEX_SCALE = 4.0
OPTICAL_DEPTH = 4.0
LOG2_E = 1.4426950408889634
TINY = 1.2e-38
FIELD = 13
UNIT = 4096.0
MIB = 1024 * 1024
F32 = jnp.float32
BF16 = jnp.bfloat16


def parity():
    return lax.rem(lax.axis_index("depth"), 2)


def stencil(ahead, behind):
    return 45.0 * (ahead[0] - behind[0]) - 9.0 * (ahead[1] - behind[1]) + (ahead[2] - behind[2])


def weight_of(distance):
    out = jnp.zeros(distance.shape, F32)
    for k, weight in ((1, 45.0), (2, -9.0), (3, 1.0)):
        out = jnp.where(distance == k, weight, out)
        out = jnp.where(distance == -k, -weight, out)
    return out


def halves(x):
    high = x.astype(BF16)
    low = (x - high.astype(F32)).astype(BF16)
    return jnp.concatenate([high, low], axis=1)


def ends_kernel(vel, far, near, sems):
    odd = parity()
    last = vel.shape[1] - REACH
    copies = [
        pltpu.make_async_copy(vel.at[:, pl.ds(odd * last, REACH)], far, sems.at[0]),
        pltpu.make_async_copy(vel.at[:, pl.ds((1 - odd) * last, REACH)], near, sems.at[1]),
    ]
    for copy in copies:
        copy.start()
    for copy in copies:
        copy.wait()


def edges_kernel(vel, ext, right_out, left_out, sem):
    slab, ny, cx = vel.shape[1:]
    half = ny // 2
    body = pl.ds(SUB, ny)
    copy = pltpu.make_async_copy(vel, ext.at[:, pl.ds(REACH, slab), body, :], sem.at[0])
    copy.start()
    zero = jnp.zeros((SUB, cx), F32)
    for c in range(3):
        for z in range(slab):
            ext[c, REACH + z, pl.ds(0, SUB), :] = zero
            ext[c, REACH + z, pl.ds(ny + SUB, SUB), :] = zero
        for z in range(REACH):
            ext[c, z, body, :] = jnp.zeros((ny, cx), F32)
            ext[c, REACH + slab + z, body, :] = jnp.zeros((ny, cx), F32)
    lane = lax.broadcasted_iota(jnp.int32, (SUB, cx), 1)

    def tile(t, _):
        for c in range(3):
            to_right = jnp.zeros((SUB, cx), F32)
            to_left = jnp.zeros((SUB, cx), F32)
            for z in range(slab):
                for h in range(2):
                    first = GROUP * z + 4 * h
                    rows = pl.ds(pl.multiple_of(h * half + t * SUB, SUB), SUB)
                    turned = pltpu.roll(vel[c, z, rows, :], (first + REACH) % cx, 1)
                    to_right = jnp.where((lane >= first) & (lane < first + 4), turned, to_right)
                    place = lax.rem(lane + (2 * cx - first - REACH), cx)
                    to_left = jnp.where(place < 4, turned, to_left)
            rows = pl.ds(pl.multiple_of(t * SUB, SUB), SUB)
            right_out[c, rows, :] = to_right
            left_out[c, rows, :] = to_left
        return 0

    lax.fori_loop(0, half // SUB, tile, 0)
    copy.wait()


def slopes_kernel(ext, near, metric, stream, span, outline, band):
    slab, ny, cx = stream.shape[1:]
    odd = parity()
    body = pl.ds(SUB, ny)
    source = lax.broadcasted_iota(jnp.int32, (cx, cx), 0)
    target = lax.broadcasted_iota(jnp.int32, (cx, cx), 1)
    weights = weight_of(source - target).astype(BF16)
    band[pl.ds(0, cx), :] = weights
    band[pl.ds(cx, cx), :] = weights
    row = lax.broadcasted_iota(jnp.int32, (SUB, cx), 0)
    sign = jnp.full((SUB, cx), 1 - 2 * odd, jnp.int32).astype(F32)
    reach = [45.0 * sign, -9.0 * sign, sign]
    steps = math.gcd(slab, ny // SUB)
    layers = slab // steps
    tiles = ny // SUB // steps

    def along(z):
        rows = jnp.concatenate([halves(ext[c, REACH + z, body, :]) for c in range(3)], axis=0)
        out = jnp.dot(rows, band[...], preferred_element_type=F32)
        for c in range(3):
            stream[c, z] = out[c * ny : (c + 1) * ny]

    def tile(t):
        base = pl.multiple_of(t * SUB, SUB)
        rows = pl.ds(base, SUB)
        inner = pl.ds(base + SUB, SUB)
        scale = jnp.zeros((SUB, cx), F32)
        for r in range(SUB):
            scale = jnp.where(row == r, metric[base + r], scale)

        def slopes(z):
            dy = [
                scale * stencil(
                    [ext[c, REACH + z, pl.ds(base + SUB + k, SUB), :] for k in (1, 2, 3)],
                    [ext[c, REACH + z, pl.ds(base + SUB - k, SUB), :] for k in (1, 2, 3)],
                )
                for c in range(3)
            ]
            dz = [
                stencil(
                    [ext[c, REACH + z + k, inner, :] for k in (1, 2, 3)],
                    [ext[c, REACH + z - k, inner, :] for k in (1, 2, 3)],
                )
                for c in range(3)
            ]
            return dy, dz

        def keep(z, dy, dz):
            turn = dy[2] - dz[1]
            span[0, z, rows, :] = dy[0]
            span[1, z, rows, :] = dz[0]
            span[2, z, rows, :] = dy[1] * dy[1] + dz[2] * dz[2] + 2.0 * (dy[2] * dz[1])
            span[3, z, rows, :] = turn * turn

        for z in range(REACH, slab - REACH):
            keep(z, *slopes(z))
        beyond = [[near[c, odd * (2 - 2 * r) + r, rows, :] for r in range(REACH)] for c in range(3)]
        for q in range(REACH):
            low, high = q, slab - 1 - q
            z = odd * (low - high) + high
            dy, dz = slopes(z)
            for c in range(3):
                for r in range(REACH - q):
                    dz[c] = dz[c] + reach[q + r] * beyond[c][r]
            keep(z, dy, dz)
            dy, dz = slopes(odd * (high - low) + low)
            for c in range(3):
                outline[c, q, rows, :] = dy[c]
                outline[3 + c, q, rows, :] = dz[c]

    def step(s, _):
        for k in range(layers):
            along(s * layers + k)
        for k in range(tiles):
            tile(s * tiles + k)
        return 0

    lax.fori_loop(0, steps, step, 0)


def tables(colour_map):
    bins = colour_map.shape[1]
    table = colour_map[...].astype(F32) * UNIT
    after = pltpu.roll(table, bins - 1, 1)
    packed = table.astype(jnp.int32) * (1 << FIELD) + after.astype(jnp.int32)
    return [jnp.broadcast_to(packed[k : k + 1], (SUB, bins)) for k in range(4)]


def shade(square, spin, seen, pairs, total_depth):
    bins = pairs[0].shape[1]
    half_top = (bins - 1) * 0.5
    level = half_top + half_top * jnp.tanh(square * (-0.5 / (3600.0 * CRITERION_SCALE)))
    low = jnp.minimum(jnp.floor(level), bins - 2.0)
    fraction = level - low
    index = low.astype(jnp.int32)

    def value(k):
        pair = jnp.take_along_axis(pairs[k], index, axis=1)
        first = lax.shift_right_logical(pair, FIELD).astype(F32)
        second = (pair & ((1 << FIELD) - 1)).astype(F32)
        return first + fraction * (second - first)

    gain = -LOG2_E * OPTICAL_DEPTH / (total_depth * UNIT)
    passed = jnp.exp2(jnp.where(seen, value(0) * gain, 0.0))
    length = spin * lax.rsqrt(jnp.maximum(spin, TINY))
    strength = jnp.tanh(length * (1.0 / (60.0 * VORTEX_SCALE)))
    return passed, [value(k) for k in (1, 2, 3)], strength


def inner_kernel(
    total_depth, stream, span, from_left, from_right, counts, colour_map,
    part, stream_out, along, packed, place,
):
    slab, ny, cx = stream.shape[1:]
    half = ny // 2
    odd = parity()
    lane = lax.broadcasted_iota(jnp.int32, (SUB, cx), 1)
    within = lax.rem(lane, GROUP)

    def pack(t, _):
        rows = pl.ds(pl.multiple_of(2 * t * SUB, 2 * SUB), 2 * SUB)
        wide = lax.rem(lax.broadcasted_iota(jnp.int32, (2 * SUB, cx), 1), GROUP)
        for c in range(3):
            right = from_left[c, rows, :]
            left = from_right[c, rows, :]
            first = jnp.where(wide < 3, right, left)
            second = pltpu.roll(jnp.where((wide >= 4) & (wide < 7), right, left), cx - 4, 1)
            at = pl.multiple_of(c * ny + 2 * t * SUB, 2 * SUB)
            packed[pl.ds(at, 2 * SUB), :] = halves(first)
            packed[pl.ds(pl.multiple_of(at + half, 2 * SUB), 2 * SUB), :] = halves(second)
        return 0

    lax.fori_loop(0, half // (2 * SUB), pack, 0)
    place[...] = jnp.zeros(place.shape, F32)
    source = lax.broadcasted_iota(jnp.int32, (SUB, cx), 0)
    column = jnp.where(source < REACH, source - REACH, source - REACH + cx)
    weights = weight_of(column - lane)
    place[pl.ds(cx, SUB), :] = jnp.where(source < 2 * REACH, weights, 0.0)

    together = math.gcd(slab, 4)

    def layers(s, _):
        spread = jnp.concatenate(
            [
                place[pl.ds(pl.multiple_of(cx - GROUP * (s * together + k), SUB), cx), :].astype(BF16)
                for k in range(together)
            ],
            axis=1,
        )
        add = jnp.dot(
            packed[...], jnp.concatenate([spread, spread], axis=0), preferred_element_type=F32
        )
        for k in range(together):
            z = s * together + k
            for c in range(3):
                along[c, z] = stream[c, z] + add[c * ny : (c + 1) * ny, k * cx : (k + 1) * cx]
        return 0

    lax.fori_loop(0, slab // together, layers, 0)
    for q in range(REACH):
        z = odd * (slab - 1 - 2 * q) + q
        for c in range(3):
            stream_out[c, q] = along[c, z]

    pairs = tables(colour_map)
    start = REACH * (1 - odd)
    first_depth = lax.axis_index("depth") * slab + start

    def tile(t, _):
        rows = pl.ds(pl.multiple_of(t * SUB, SUB), SUB)
        count = counts[rows, :] - first_depth
        colour = [jnp.zeros((SUB, cx), F32) for _ in range(3)]
        clear = jnp.ones((SUB, cx), F32)
        for cell in range(slab - REACH):
            dx = [along[c, start + cell, rows, :] for c in range(3)]
            dy, dz, rest, turn = [span[k, start + cell, rows, :] for k in range(4)]
            square = rest + dx[0] * dx[0] + 2.0 * (dy * dx[1] + dz * dx[2])
            w1 = dz - dx[2]
            w2 = dx[1] - dy
            spin = turn + w1 * w1 + w2 * w2
            passed, values, strength = shade(square, spin, count > cell, pairs, total_depth)
            after = clear * passed
            weight = (clear - after) * strength
            colour = [colour[k] + weight * values[k] for k in range(3)]
            clear = after
        for k in range(3):
            part[k, rows, :] = colour[k] * (1.0 / UNIT)
        part[3, rows, :] = clear
        return 0

    lax.fori_loop(0, ny // SUB, tile, 0)


def outer_kernel(
    total_depth, far, outline, stream, part, counts, colour_map, mine, theirs, whole
):
    ny, cx = counts.shape
    odd = parity()
    pairs = tables(colour_map)
    slab = total_depth // lax.axis_size("depth")
    slab_first = lax.axis_index("depth") * slab
    sign = jnp.full((SUB, cx), 2 * odd - 1, jnp.int32).astype(F32)
    front = jnp.full((SUB, cx), odd, jnp.int32) == 0
    weights = [45.0 * sign, -9.0 * sign, sign]

    def tile(t, _):
        rows = pl.ds(pl.multiple_of(t * SUB, SUB), SUB)
        count = counts[rows, :] - slab_first
        beyond = [
            [far[c, (1 - odd) * (2 - 2 * r) + r, rows, :] for r in range(REACH)] for c in range(3)
        ]
        layers = []
        for q in range(REACH):
            dx = [stream[c, q, rows, :] for c in range(3)]
            dy = [outline[c, q, rows, :] for c in range(3)]
            dz = [outline[3 + c, q, rows, :] for c in range(3)]
            for c in range(3):
                for r in range(REACH - q):
                    dz[c] = dz[c] + weights[q + r] * beyond[c][r]
            w0 = dy[2] - dz[1]
            w1 = dz[0] - dx[2]
            w2 = dx[1] - dy[0]
            square = dx[0] * dx[0] + dy[1] * dy[1] + dz[2] * dz[2]
            square = square + 2.0 * (dy[0] * dx[1] + dz[0] * dx[2] + dz[1] * dy[2])
            spin = w0 * w0 + w1 * w1 + w2 * w2
            seen = count > odd * (slab - 1 - 2 * q) + q
            passed, values, strength = shade(square, spin, seen, pairs, total_depth)
            weight = (1.0 - passed) * (strength * (1.0 / UNIT))
            layers.append([weight * value for value in values] + [passed])
        first = [jnp.where(front, a, b) for a, b in zip(layers[0], layers[2])]
        last = [jnp.where(front, b, a) for a, b in zip(layers[0], layers[2])]
        clear = first[3] * layers[1][3]
        rest = part[3, rows, :]
        outer_clear = clear * last[3]
        for k in range(3):
            own = first[k] + first[3] * layers[1][k] + clear * last[k]
            inner = part[k, rows, :]
            whole[k, rows, :] = jnp.where(front, own + outer_clear * inner, inner + rest * own)
        whole[3, rows, :] = 1.0 - outer_clear * rest
        return 0

    lax.fori_loop(0, ny // SUB, tile, 0)
    chips, _, share, _ = mine.shape
    me = lax.axis_index("depth")
    for s in range(chips):
        owner = 2 * lax.rem(me // 2 + s, chips)
        for k in range(4):
            mine[s, k] = whole[k, pl.ds((owner + odd) * share, share), :]
            theirs[s, k] = whole[k, pl.ds((owner + 1 - odd) * share, share), :]


def over(front, back):
    return front + (1.0 - front[..., 3:, :, :]) * back


def gather_rays(mine, theirs):
    chips = mine.shape[0]
    devices = 2 * chips
    me = lax.axis_index("depth")
    odd = lax.rem(me, 2) == 1
    theirs = lax.ppermute(theirs, "depth", [(i, i + 1 - 2 * (i % 2)) for i in range(devices)])
    both = over(jnp.where(odd, theirs, mine), jnp.where(odd, mine, theirs))
    got = [both[0]] + [
        lax.ppermute(both[s], "depth", [(i, (i + 2 * s) % devices) for i in range(devices)])
        for s in range(1, chips)
    ]
    first = last = jnp.zeros_like(got[0])
    for s in reversed(range(chips)):
        before = me // 2 >= s
        first = over(first, jnp.where(before, got[s], 0.0))
        last = over(last, jnp.where(before, 0.0, got[s]))
    return over(first, last)


def vmem(count):
    return [pl.BlockSpec(memory_space=pltpu.VMEM)] * count


def held(*dims):
    return pltpu.VMEM(dims, F32)


def in_vmem(x):
    return pltpu.with_memory_space_constraint(x, pltpu.VMEM)


def per_device(velocity, metric, colour_map, counts):
    _, slab, ny, cx = velocity.shape
    devices = lax.axis_size("depth")
    tiles = lax.axis_size("tile")
    total_depth = slab * devices
    scalars = pl.BlockSpec(memory_space=pltpu.SMEM)

    def limit(size):
        return pltpu.CompilerParams(vmem_limit_bytes=size * MIB)

    hbm = pl.BlockSpec(memory_space=pltpu.HBM)
    ends = (3, REACH, ny, cx)
    padded = (3, slab + 2 * REACH, ny + 2 * SUB, cx)
    columns = (3, ny // 2, cx)
    up = [(i, (i + 1) % devices) for i in range(devices)]
    down = [(i, (i - 1) % devices) for i in range(devices)]
    whole = pltpu.with_memory_space_constraint(velocity, pltpu.HBM)
    far, near = pl.pallas_call(
        ends_kernel,
        out_shape=(pltpu.VMEM(ends, F32), pltpu.VMEM(ends, F32)),
        in_specs=[hbm],
        out_specs=tuple(vmem(2)),
        scratch_shapes=[pltpu.SemaphoreType.DMA((2,))],
        compiler_params=limit(4),
        name="ends",
    )(whole)
    near = lax.ppermute(near, "depth", [(down if i % 2 else up)[i] for i in range(devices)])
    far = lax.ppermute(far, "depth", [(up if i % 2 else down)[i] for i in range(devices)])

    ext, to_right, to_left = pl.pallas_call(
        edges_kernel,
        out_shape=(pltpu.VMEM(padded, F32), pltpu.VMEM(columns, F32), pltpu.VMEM(columns, F32)),
        in_specs=vmem(1),
        out_specs=tuple(vmem(3)),
        scratch_shapes=[pltpu.SemaphoreType.DMA((1,))],
        compiler_params=limit(4),
        name="edges",
    )(velocity)
    from_left = lax.ppermute(to_right, "tile", [(i, (i + 1) % tiles) for i in range(tiles)])
    from_right = lax.ppermute(to_left, "tile", [(i, (i - 1) % tiles) for i in range(tiles)])

    stream, span, outline = pl.pallas_call(
        slopes_kernel,
        out_shape=(
            held(3, slab, ny, cx),
            held(4, slab, ny, cx),
            held(6, REACH, ny, cx),
        ),
        in_specs=vmem(2) + [scalars],
        out_specs=tuple(vmem(3)),
        scratch_shapes=[pltpu.VMEM((2 * cx, cx), BF16)],
        compiler_params=limit(4),
        name="slopes",
    )(in_vmem(ext), in_vmem(near), metric)

    part, stream = pl.pallas_call(
        functools.partial(inner_kernel, total_depth),
        out_shape=(held(4, ny, cx), held(3, REACH, ny, cx)),
        in_specs=vmem(6),
        out_specs=tuple(vmem(2)),
        scratch_shapes=[
            pltpu.VMEM((3, slab, ny, cx), F32),
            pltpu.VMEM((3 * ny, 2 * cx), BF16),
            pltpu.VMEM((2 * cx, cx), F32),
        ],
        compiler_params=limit(8),
        name="inner",
    )(*map(in_vmem, (stream, span, from_left, from_right, counts, colour_map)))

    piece = held(devices // 2, 4, ny // devices, cx)
    mine, theirs = pl.pallas_call(
        functools.partial(outer_kernel, total_depth),
        out_shape=(piece, piece),
        in_specs=vmem(6),
        out_specs=tuple(vmem(2)),
        scratch_shapes=[pltpu.VMEM((4, ny, cx), F32)],
        compiler_params=limit(4),
        name="outer",
    )(*map(in_vmem, (far, outline, stream, part, counts, colour_map)))
    return gather_rays(mine, theirs)


def solution(mesh):
    in_specs = (P(None, "depth", None, "tile"), P(), P(), P(None, "tile"))
    out_specs = P(None, "depth", "tile")
    return jax.shard_map(
        per_device, mesh=mesh, in_specs=in_specs, out_specs=out_specs, check_vma=False
    )
```

```python
import functools
import math

import jax
import jax.numpy as jnp
from jax import lax
from jax.experimental import pallas as pl
from jax.experimental.pallas import tpu as pltpu
from jax.sharding import PartitionSpec as P

REACH = 3
SUB = 8
GROUP = 8
CRITERION_SCALE = 2.0
VORTEX_SCALE = 4.0
OPTICAL_DEPTH = 4.0
LOG2_E = 1.4426950408889634
TINY = 1.2e-38
FIELD = 13
UNIT = 4096.0
MIB = 1024 * 1024
F32 = jnp.float32
BF16 = jnp.bfloat16


def parity():
    return lax.rem(lax.axis_index("depth"), 2)


def stencil(ahead, behind):
    return 45.0 * (ahead[0] - behind[0]) - 9.0 * (ahead[1] - behind[1]) + (ahead[2] - behind[2])


def weight_of(distance):
    out = jnp.zeros(distance.shape, F32)
    for k, weight in ((1, 45.0), (2, -9.0), (3, 1.0)):
        out = jnp.where(distance == k, weight, out)
        out = jnp.where(distance == -k, -weight, out)
    return out


def halves(x):
    high = x.astype(BF16)
    low = (x - high.astype(F32)).astype(BF16)
    return jnp.concatenate([high, low], axis=1)


def ends_kernel(vel, near, far, sems):
    odd = parity()
    last = vel.shape[1] - REACH
    rows = pl.ds(0, vel.shape[2])
    copies = [
        pltpu.make_async_copy(
            vel.at[:, pl.ds(odd * last, REACH)], far.at[:, :, rows, :], sems.at[0]),
        pltpu.make_async_copy(vel.at[:, pl.ds((1 - odd) * last, REACH)], near, sems.at[1]),
    ]
    for copy in copies:
        copy.start()
    for copy in copies:
        copy.wait()


def edges_kernel(vel, ext, right_out, left_out, sem):
    slab, ny, cx = vel.shape[1:]
    half = ny // 2
    body = pl.ds(SUB, ny)
    copy = pltpu.make_async_copy(vel, ext.at[:, pl.ds(REACH, slab), body, :], sem.at[0])
    copy.start()
    zero = jnp.zeros((SUB, cx), F32)
    for c in range(3):
        for z in range(slab):
            ext[c, REACH + z, pl.ds(0, SUB), :] = zero
            ext[c, REACH + z, pl.ds(ny + SUB, SUB), :] = zero
        for z in range(REACH):
            ext[c, z, body, :] = jnp.zeros((ny, cx), F32)
            ext[c, REACH + slab + z, body, :] = jnp.zeros((ny, cx), F32)
    lane = lax.broadcasted_iota(jnp.int32, (SUB, cx), 1)

    def tile(t, _):
        for c in range(3):
            to_right = jnp.zeros((SUB, cx), F32)
            to_left = jnp.zeros((SUB, cx), F32)
            for z in range(slab):
                for h in range(2):
                    first = GROUP * z + 4 * h
                    rows = pl.ds(pl.multiple_of(h * half + t * SUB, SUB), SUB)
                    turned = pltpu.roll(vel[c, z, rows, :], (first + REACH) % cx, 1)
                    to_right = jnp.where((lane >= first) & (lane < first + 4), turned, to_right)
                    place = lax.rem(lane + (2 * cx - first - REACH), cx)
                    to_left = jnp.where(place < 4, turned, to_left)
            rows = pl.ds(pl.multiple_of(t * SUB, SUB), SUB)
            right_out[c, rows, :] = to_right
            left_out[c, rows, :] = to_left
        return 0

    lax.fori_loop(0, half // SUB, tile, 0)
    copy.wait()


def slopes_kernel(ext, near, metric, stream, span, outline, band):
    slab, ny, cx = stream.shape[1:]
    odd = parity()
    body = pl.ds(SUB, ny)
    source = lax.broadcasted_iota(jnp.int32, (cx, cx), 0)
    target = lax.broadcasted_iota(jnp.int32, (cx, cx), 1)
    weights = weight_of(source - target).astype(BF16)
    band[pl.ds(0, cx), :] = weights
    band[pl.ds(cx, cx), :] = weights
    row = lax.broadcasted_iota(jnp.int32, (SUB, cx), 0)
    sign = jnp.full((SUB, cx), 1 - 2 * odd, jnp.int32).astype(F32)
    reach = [45.0 * sign, -9.0 * sign, sign]
    steps = math.gcd(slab, ny // SUB)
    layers = slab // steps
    tiles = ny // SUB // steps

    def along(z):
        rows = jnp.concatenate([halves(ext[c, REACH + z, body, :]) for c in range(3)], axis=0)
        out = jnp.dot(rows, band[...], preferred_element_type=F32)
        for c in range(3):
            stream[c, z] = out[c * ny : (c + 1) * ny]

    def tile(t):
        base = pl.multiple_of(t * SUB, SUB)
        rows = pl.ds(base, SUB)
        inner = pl.ds(base + SUB, SUB)
        scale = jnp.zeros((SUB, cx), F32)
        for r in range(SUB):
            scale = jnp.where(row == r, metric[base + r], scale)

        def slopes(z):
            dy = [
                scale * stencil(
                    [ext[c, REACH + z, pl.ds(base + SUB + k, SUB), :] for k in (1, 2, 3)],
                    [ext[c, REACH + z, pl.ds(base + SUB - k, SUB), :] for k in (1, 2, 3)],
                )
                for c in range(3)
            ]
            dz = [
                stencil(
                    [ext[c, REACH + z + k, inner, :] for k in (1, 2, 3)],
                    [ext[c, REACH + z - k, inner, :] for k in (1, 2, 3)],
                )
                for c in range(3)
            ]
            return dy, dz

        def keep(z, dy, dz):
            turn = dy[2] - dz[1]
            span[0, z, rows, :] = dy[0]
            span[1, z, rows, :] = dz[0]
            span[2, z, rows, :] = dy[1] * dy[1] + dz[2] * dz[2] + 2.0 * (dy[2] * dz[1])
            span[3, z, rows, :] = turn * turn

        for z in range(REACH, slab - REACH):
            keep(z, *slopes(z))
        beyond = [[near[c, odd * (2 - 2 * r) + r, rows, :] for r in range(REACH)] for c in range(3)]
        for q in range(REACH):
            low, high = q, slab - 1 - q
            z = odd * (low - high) + high
            dy, dz = slopes(z)
            for c in range(3):
                for r in range(REACH - q):
                    dz[c] = dz[c] + reach[q + r] * beyond[c][r]
            keep(z, dy, dz)
            dy, dz = slopes(odd * (high - low) + low)
            for c in range(3):
                outline[c, q, rows, :] = dy[c]
                outline[3 + c, q, rows, :] = dz[c]

    def step(s, _):
        for k in range(layers):
            along(s * layers + k)
        for k in range(tiles):
            tile(s * tiles + k)
        return 0

    lax.fori_loop(0, steps, step, 0)


def tables(colour_map):
    bins = colour_map.shape[1]
    table = colour_map[...].astype(F32) * UNIT
    after = pltpu.roll(table, bins - 1, 1)
    packed = table.astype(jnp.int32) * (1 << FIELD) + after.astype(jnp.int32)
    return [jnp.broadcast_to(packed[k : k + 1], (SUB, bins)) for k in range(4)]


def shade(square, spin, seen, pairs, total_depth):
    bins = pairs[0].shape[1]
    half_top = (bins - 1) * 0.5
    level = half_top + half_top * jnp.tanh(square * (-0.5 / (3600.0 * CRITERION_SCALE)))
    low = jnp.minimum(jnp.floor(level), bins - 2.0)
    fraction = level - low
    index = low.astype(jnp.int32)

    def value(k):
        pair = jnp.take_along_axis(pairs[k], index, axis=1)
        first = lax.shift_right_logical(pair, FIELD).astype(F32)
        second = (pair & ((1 << FIELD) - 1)).astype(F32)
        return first + fraction * (second - first)

    gain = -LOG2_E * OPTICAL_DEPTH / (total_depth * UNIT)
    passed = jnp.exp2(jnp.where(seen, value(0) * gain, 0.0))
    length = spin * lax.rsqrt(jnp.maximum(spin, TINY))
    strength = jnp.tanh(length * (1.0 / (60.0 * VORTEX_SCALE)))
    return passed, [value(k) for k in (1, 2, 3)], strength


def inner_kernel(
    total_depth, stream, span, from_left, from_right, counts, colour_map,
    part, stream_out, along, packed, place,
):
    slab, ny, cx = stream.shape[1:]
    half = ny // 2
    odd = parity()
    lane = lax.broadcasted_iota(jnp.int32, (SUB, cx), 1)
    within = lax.rem(lane, GROUP)

    def pack(t, _):
        rows = pl.ds(pl.multiple_of(2 * t * SUB, 2 * SUB), 2 * SUB)
        wide = lax.rem(lax.broadcasted_iota(jnp.int32, (2 * SUB, cx), 1), GROUP)
        for c in range(3):
            right = from_left[c, rows, :]
            left = from_right[c, rows, :]
            first = jnp.where(wide < 3, right, left)
            second = pltpu.roll(jnp.where((wide >= 4) & (wide < 7), right, left), cx - 4, 1)
            at = pl.multiple_of(c * ny + 2 * t * SUB, 2 * SUB)
            packed[pl.ds(at, 2 * SUB), :] = halves(first)
            packed[pl.ds(pl.multiple_of(at + half, 2 * SUB), 2 * SUB), :] = halves(second)
        return 0

    lax.fori_loop(0, half // (2 * SUB), pack, 0)
    place[...] = jnp.zeros(place.shape, F32)
    source = lax.broadcasted_iota(jnp.int32, (SUB, cx), 0)
    column = jnp.where(source < REACH, source - REACH, source - REACH + cx)
    weights = weight_of(column - lane)
    place[pl.ds(cx, SUB), :] = jnp.where(source < 2 * REACH, weights, 0.0)

    together = math.gcd(slab, 4)

    def layers(s, _):
        spread = jnp.concatenate(
            [
                place[pl.ds(pl.multiple_of(cx - GROUP * (s * together + k), SUB), cx), :].astype(BF16)
                for k in range(together)
            ],
            axis=1,
        )
        add = jnp.dot(
            packed[...], jnp.concatenate([spread, spread], axis=0), preferred_element_type=F32
        )
        for k in range(together):
            z = s * together + k
            for c in range(3):
                along[c, z] = stream[c, z] + add[c * ny : (c + 1) * ny, k * cx : (k + 1) * cx]
        return 0

    lax.fori_loop(0, slab // together, layers, 0)
    for q in range(REACH):
        z = odd * (slab - 1 - 2 * q) + q
        for c in range(3):
            stream_out[c, q, pl.ds(0, ny), :] = along[c, z]

    pairs = tables(colour_map)
    start = REACH * (1 - odd)
    first_depth = lax.axis_index("depth") * slab + start

    def tile(t, _):
        rows = pl.ds(pl.multiple_of(t * SUB, SUB), SUB)
        count = counts[rows, :] - first_depth
        colour = [jnp.zeros((SUB, cx), F32) for _ in range(3)]
        clear = jnp.ones((SUB, cx), F32)
        for cell in range(slab - REACH):
            dx = [along[c, start + cell, rows, :] for c in range(3)]
            dy, dz, rest, turn = [span[k, start + cell, rows, :] for k in range(4)]
            square = rest + dx[0] * dx[0] + 2.0 * (dy * dx[1] + dz * dx[2])
            w1 = dz - dx[2]
            w2 = dx[1] - dy
            spin = turn + w1 * w1 + w2 * w2
            passed, values, strength = shade(square, spin, count > cell, pairs, total_depth)
            after = clear * passed
            weight = (clear - after) * strength
            colour = [colour[k] + weight * values[k] for k in range(3)]
            clear = after
        for k in range(3):
            part[k, rows, :] = colour[k] * (1.0 / UNIT)
        part[3, rows, :] = clear
        return 0

    lax.fori_loop(0, ny // SUB, tile, 0)


def outer_kernel(total_depth, own, far, outline, stream, part, counts, colour_map, out):
    chips, _, share, cx = out.shape
    odd = parity()
    me = lax.axis_index("depth")
    slab = total_depth // lax.axis_size("depth")
    pairs = tables(colour_map)
    sign = jnp.full((SUB, cx), 2 * odd - 1, jnp.int32).astype(F32)
    front = jnp.full((SUB, cx), odd, jnp.int32) == 0
    weights = [45.0 * sign, -9.0 * sign, sign]

    def window(rows):
        count = counts[rows, :] - me * slab
        beyond = [
            [far[c, (1 - odd) * (2 - 2 * r) + r, rows, :] for r in range(REACH)]
            for c in range(3)
        ]
        layers = []
        for q in range(REACH):
            dx = [stream[c, q, rows, :] for c in range(3)]
            dy = [outline[c, q, rows, :] for c in range(3)]
            dz = [outline[3 + c, q, rows, :] for c in range(3)]
            for c in range(3):
                for r in range(REACH - q):
                    dz[c] = dz[c] + weights[q + r] * beyond[c][r]
            w0 = dy[2] - dz[1]
            w1 = dz[0] - dx[2]
            w2 = dx[1] - dy[0]
            square = dx[0] * dx[0] + dy[1] * dy[1] + dz[2] * dz[2]
            square = square + 2.0 * (dy[0] * dx[1] + dz[0] * dx[2] + dz[1] * dy[2])
            spin = w0 * w0 + w1 * w1 + w2 * w2
            seen = count > odd * (slab - 1 - 2 * q) + q
            passed, values, strength = shade(square, spin, seen, pairs, total_depth)
            weight = (1.0 - passed) * (strength * (1.0 / UNIT))
            layers.append([weight * value for value in values] + [passed])
        first = [jnp.where(front, a, b) for a, b in zip(layers[0], layers[2])]
        last = [jnp.where(front, b, a) for a, b in zip(layers[0], layers[2])]
        clear = first[3] * layers[1][3]
        rest = part[3, rows, :]
        outer_clear = clear * last[3]
        image = []
        for k in range(3):
            edge = first[k] + first[3] * layers[1][k] + clear * last[k]
            inner = part[k, rows, :]
            image.append(jnp.where(front, edge + outer_clear * inner, inner + rest * edge))
        return image + [1.0 - outer_clear * rest]

    owner = odd if own else 1 - odd
    starts = sorted({min(w, max(share - SUB, 0)) for w in range(0, share, SUB)})
    height = min(share, SUB)
    for s in range(chips):
        chip = lax.rem(me // 2 + s, chips)
        for w in starts:
            row = (2 * chip + owner) * share + w
            image = window(pl.ds(row, SUB))
            for k in range(4):
                out[s, k, pl.ds(w, height), :] = image[k][:height]


def over(front, back):
    return front + (1.0 - front[..., 3:, :, :]) * back


def gather_rays(mine, theirs):
    chips = mine.shape[0]
    devices = 2 * chips
    me = lax.axis_index("depth")
    odd = lax.rem(me, 2) == 1
    theirs = lax.ppermute(theirs, "depth", [(i, i + 1 - 2 * (i % 2)) for i in range(devices)])
    both = over(jnp.where(odd, theirs, mine), jnp.where(odd, mine, theirs))
    got = [both[0]] + [
        lax.ppermute(both[s], "depth", [(i, (i + 2 * s) % devices) for i in range(devices)])
        for s in range(1, chips)
    ]
    first = last = jnp.zeros_like(got[0])
    for s in reversed(range(chips)):
        before = me // 2 >= s
        first = over(first, jnp.where(before, got[s], 0.0))
        last = over(last, jnp.where(before, 0.0, got[s]))
    return over(first, last)


def vmem(count):
    return [pl.BlockSpec(memory_space=pltpu.VMEM)] * count


def held(*dims):
    return pltpu.VMEM(dims, F32)


def in_vmem(x):
    return pltpu.with_memory_space_constraint(x, pltpu.VMEM)


def per_device(velocity, metric, colour_map, counts):
    _, slab, ny, cx = velocity.shape
    devices = lax.axis_size("depth")
    tiles = lax.axis_size("tile")
    total_depth = slab * devices
    scalars = pl.BlockSpec(memory_space=pltpu.SMEM)

    def limit(size):
        return pltpu.CompilerParams(vmem_limit_bytes=size * MIB)

    hbm = pl.BlockSpec(memory_space=pltpu.HBM)
    share = ny // devices
    spare = SUB if share < SUB else 0
    padded = (3, slab + 2 * REACH, ny + 2 * SUB, cx)
    columns = (3, ny // 2, cx)
    up = [(i, (i + 1) % devices) for i in range(devices)]
    down = [(i, (i - 1) % devices) for i in range(devices)]
    whole = pltpu.with_memory_space_constraint(velocity, pltpu.HBM)
    near, far = pl.pallas_call(
        ends_kernel,
        out_shape=(held(3, REACH, ny, cx), held(3, REACH, ny + spare, cx)),
        in_specs=[hbm],
        out_specs=tuple(vmem(2)),
        scratch_shapes=[pltpu.SemaphoreType.DMA((2,))],
        compiler_params=limit(4),
        name="ends",
    )(whole)
    near = lax.ppermute(near, "depth", [(down if i % 2 else up)[i] for i in range(devices)])
    far = lax.ppermute(far, "depth", [(up if i % 2 else down)[i] for i in range(devices)])

    ext, to_right, to_left = pl.pallas_call(
        edges_kernel,
        out_shape=(held(*padded), held(*columns), held(*columns)),
        in_specs=vmem(1),
        out_specs=tuple(vmem(3)),
        scratch_shapes=[pltpu.SemaphoreType.DMA((1,))],
        compiler_params=limit(4),
        name="edges",
    )(velocity)
    from_left = lax.ppermute(to_right, "tile", [(i, (i + 1) % tiles) for i in range(tiles)])
    from_right = lax.ppermute(to_left, "tile", [(i, (i - 1) % tiles) for i in range(tiles)])

    stream, span, outline = pl.pallas_call(
        slopes_kernel,
        out_shape=(
            held(3, slab, ny, cx),
            held(4, slab, ny, cx),
            held(6, REACH, ny + spare, cx),
        ),
        in_specs=vmem(2) + [scalars],
        out_specs=tuple(vmem(3)),
        scratch_shapes=[pltpu.VMEM((2 * cx, cx), BF16)],
        compiler_params=limit(4),
        name="slopes",
    )(in_vmem(ext), in_vmem(near), metric)

    part, stream = pl.pallas_call(
        functools.partial(inner_kernel, total_depth),
        out_shape=(held(4, ny + spare, cx), held(3, REACH, ny + spare, cx)),
        in_specs=vmem(6),
        out_specs=tuple(vmem(2)),
        scratch_shapes=[
            pltpu.VMEM((3, slab, ny, cx), F32),
            pltpu.VMEM((3 * ny, 2 * cx), BF16),
            pltpu.VMEM((2 * cx, cx), F32),
        ],
        compiler_params=limit(8),
        name="inner",
    )(*map(in_vmem, (stream, span, from_left, from_right, counts, colour_map)))

    tall = jnp.pad(counts, ((0, spare), (0, 0))) if spare else counts
    rest = tuple(map(in_vmem, (far, outline, stream, part, tall, colour_map)))

    def outer(own, name):
        return pl.pallas_call(
            functools.partial(outer_kernel, total_depth, own),
            out_shape=held(devices // 2, 4, share, cx),
            in_specs=vmem(6),
            out_specs=vmem(1)[0],
            compiler_params=limit(4),
            name=name,
        )(*rest)

    theirs = outer(False, "theirs")
    return gather_rays(outer(True, "mine"), theirs)


def solution(mesh):
    in_specs = (P(None, "depth", None, "tile"), P(), P(), P(None, "tile"))
    out_specs = P(None, "depth", "tile")
    return jax.shard_map(
        per_device, mesh=mesh, in_specs=in_specs, out_specs=out_specs, check_vma=False
    )
```

```python
import functools
import math

import jax
import jax.numpy as jnp
from jax import lax
from jax.experimental import pallas as pl
from jax.experimental.pallas import tpu as pltpu
from jax.sharding import PartitionSpec as P

REACH = 3
SUB = 8
GROUP = 8
CRITERION_SCALE = 2.0
VORTEX_SCALE = 4.0
OPTICAL_DEPTH = 4.0
LOG2_E = 1.4426950408889634
TINY = 1.2e-38
FIELD = 13
UNIT = 4096.0
MIB = 1024 * 1024
F32 = jnp.float32
BF16 = jnp.bfloat16


def parity():
    return lax.rem(lax.axis_index("depth"), 2)


def stencil(ahead, behind):
    return 45.0 * (ahead[0] - behind[0]) - 9.0 * (ahead[1] - behind[1]) + (ahead[2] - behind[2])


def weight_of(distance):
    out = jnp.zeros(distance.shape, F32)
    for k, weight in ((1, 45.0), (2, -9.0), (3, 1.0)):
        out = jnp.where(distance == k, weight, out)
        out = jnp.where(distance == -k, -weight, out)
    return out


def halves(x):
    high = x.astype(BF16)
    low = (x - high.astype(F32)).astype(BF16)
    return jnp.concatenate([high, low], axis=1)


def ends_kernel(vel, near, far, sems):
    odd = parity()
    last = vel.shape[1] - REACH
    rows = pl.ds(0, vel.shape[2])
    copies = [
        pltpu.make_async_copy(
            vel.at[:, pl.ds(odd * last, REACH)], far.at[:, :, rows, :], sems.at[0]),
        pltpu.make_async_copy(vel.at[:, pl.ds((1 - odd) * last, REACH)], near, sems.at[1]),
    ]
    for copy in copies:
        copy.start()
    for copy in copies:
        copy.wait()


def edges_kernel(vel, ext, right_out, left_out, sem):
    slab, ny, cx = vel.shape[1:]
    half = ny // 2
    body = pl.ds(SUB, ny)
    copy = pltpu.make_async_copy(vel, ext.at[:, pl.ds(REACH, slab), body, :], sem.at[0])
    copy.start()
    zero = jnp.zeros((SUB, cx), F32)
    for c in range(3):
        for z in range(slab):
            ext[c, REACH + z, pl.ds(0, SUB), :] = zero
            ext[c, REACH + z, pl.ds(ny + SUB, SUB), :] = zero
        for z in range(REACH):
            ext[c, z, body, :] = jnp.zeros((ny, cx), F32)
            ext[c, REACH + slab + z, body, :] = jnp.zeros((ny, cx), F32)
    lane = lax.broadcasted_iota(jnp.int32, (SUB, cx), 1)

    def tile(t, _):
        for c in range(3):
            to_right = jnp.zeros((SUB, cx), F32)
            to_left = jnp.zeros((SUB, cx), F32)
            for z in range(slab):
                for h in range(2):
                    first = GROUP * z + 4 * h
                    rows = pl.ds(pl.multiple_of(h * half + t * SUB, SUB), SUB)
                    turned = pltpu.roll(vel[c, z, rows, :], (first + REACH) % cx, 1)
                    to_right = jnp.where((lane >= first) & (lane < first + 4), turned, to_right)
                    place = lax.rem(lane + (2 * cx - first - REACH), cx)
                    to_left = jnp.where(place < 4, turned, to_left)
            rows = pl.ds(pl.multiple_of(t * SUB, SUB), SUB)
            right_out[c, rows, :] = to_right
            left_out[c, rows, :] = to_left
        return 0

    lax.fori_loop(0, half // SUB, tile, 0)
    copy.wait()


def slopes_kernel(ext, near, metric, stream, span, outline, band):
    slab, ny, cx = stream.shape[1:]
    odd = parity()
    body = pl.ds(SUB, ny)
    source = lax.broadcasted_iota(jnp.int32, (cx, cx), 0)
    target = lax.broadcasted_iota(jnp.int32, (cx, cx), 1)
    weights = weight_of(source - target).astype(BF16)
    band[pl.ds(0, cx), :] = weights
    band[pl.ds(cx, cx), :] = weights
    row = lax.broadcasted_iota(jnp.int32, (SUB, cx), 0)
    sign = jnp.full((SUB, cx), 1 - 2 * odd, jnp.int32).astype(F32)
    reach = [45.0 * sign, -9.0 * sign, sign]
    steps = math.gcd(slab, ny // SUB)
    layers = slab // steps
    tiles = ny // SUB // steps

    def along(z):
        rows = jnp.concatenate([halves(ext[c, REACH + z, body, :]) for c in range(3)], axis=0)
        out = jnp.dot(rows, band[...], preferred_element_type=F32)
        for c in range(3):
            stream[c, z] = out[c * ny : (c + 1) * ny]

    def tile(t):
        base = pl.multiple_of(t * SUB, SUB)
        rows = pl.ds(base, SUB)
        inner = pl.ds(base + SUB, SUB)
        scale = jnp.zeros((SUB, cx), F32)
        for r in range(SUB):
            scale = jnp.where(row == r, metric[base + r], scale)

        def slopes(z):
            dy = [
                scale * stencil(
                    [ext[c, REACH + z, pl.ds(base + SUB + k, SUB), :] for k in (1, 2, 3)],
                    [ext[c, REACH + z, pl.ds(base + SUB - k, SUB), :] for k in (1, 2, 3)],
                )
                for c in range(3)
            ]
            dz = [
                stencil(
                    [ext[c, REACH + z + k, inner, :] for k in (1, 2, 3)],
                    [ext[c, REACH + z - k, inner, :] for k in (1, 2, 3)],
                )
                for c in range(3)
            ]
            return dy, dz

        def keep(z, dy, dz):
            turn = dy[2] - dz[1]
            span[0, z, rows, :] = dy[0]
            span[1, z, rows, :] = dz[0]
            span[2, z, rows, :] = dy[1] * dy[1] + dz[2] * dz[2] + 2.0 * (dy[2] * dz[1])
            span[3, z, rows, :] = turn * turn

        for z in range(REACH, slab - REACH):
            keep(z, *slopes(z))
        beyond = [[near[c, odd * (2 - 2 * r) + r, rows, :] for r in range(REACH)] for c in range(3)]
        for q in range(REACH):
            low, high = q, slab - 1 - q
            z = odd * (low - high) + high
            dy, dz = slopes(z)
            for c in range(3):
                for r in range(REACH - q):
                    dz[c] = dz[c] + reach[q + r] * beyond[c][r]
            keep(z, dy, dz)
            dy, dz = slopes(odd * (high - low) + low)
            for c in range(3):
                outline[c, q, rows, :] = dy[c]
                outline[3 + c, q, rows, :] = dz[c]

    def step(s, _):
        for k in range(layers):
            along(s * layers + k)
        for k in range(tiles):
            tile(s * tiles + k)
        return 0

    lax.fori_loop(0, steps, step, 0)


def tables(colour_map):
    bins = colour_map.shape[1]
    table = colour_map[...].astype(F32) * UNIT
    after = pltpu.roll(table, bins - 1, 1)
    packed = table.astype(jnp.int32) * (1 << FIELD) + after.astype(jnp.int32)
    return [jnp.broadcast_to(packed[k : k + 1], (SUB, bins)) for k in range(4)]


def shade(square, spin, seen, pairs, total_depth):
    bins = pairs[0].shape[1]
    half_top = (bins - 1) * 0.5
    level = half_top + half_top * jnp.tanh(square * (-0.5 / (3600.0 * CRITERION_SCALE)))
    low = jnp.minimum(jnp.floor(level), bins - 2.0)
    fraction = level - low
    index = low.astype(jnp.int32)

    def value(k):
        pair = jnp.take_along_axis(pairs[k], index, axis=1)
        first = lax.shift_right_logical(pair, FIELD).astype(F32)
        second = (pair & ((1 << FIELD) - 1)).astype(F32)
        return first + fraction * (second - first)

    gain = -LOG2_E * OPTICAL_DEPTH / (total_depth * UNIT)
    passed = jnp.exp2(jnp.where(seen, value(0) * gain, 0.0))
    length = spin * lax.rsqrt(jnp.maximum(spin, TINY))
    strength = jnp.tanh(length * (1.0 / (60.0 * VORTEX_SCALE)))
    return passed, [value(k) for k in (1, 2, 3)], strength


def inner_kernel(
    total_depth, stream, span, from_left, from_right, counts, colour_map,
    part, stream_out, terms, packed, place,
):
    slab, ny, cx = stream.shape[1:]
    half = ny // 2
    odd = parity()
    lane = lax.broadcasted_iota(jnp.int32, (SUB, cx), 1)
    within = lax.rem(lane, GROUP)

    def pack(t, _):
        rows = pl.ds(pl.multiple_of(2 * t * SUB, 2 * SUB), 2 * SUB)
        wide = lax.rem(lax.broadcasted_iota(jnp.int32, (2 * SUB, cx), 1), GROUP)
        for c in range(3):
            right = from_left[c, rows, :]
            left = from_right[c, rows, :]
            first = jnp.where(wide < 3, right, left)
            second = pltpu.roll(jnp.where((wide >= 4) & (wide < 7), right, left), cx - 4, 1)
            at = pl.multiple_of(c * ny + 2 * t * SUB, 2 * SUB)
            packed[pl.ds(at, 2 * SUB), :] = halves(first)
            packed[pl.ds(pl.multiple_of(at + half, 2 * SUB), 2 * SUB), :] = halves(second)
        return 0

    lax.fori_loop(0, half // (2 * SUB), pack, 0)
    place[...] = jnp.zeros(place.shape, F32)
    source = lax.broadcasted_iota(jnp.int32, (SUB, cx), 0)
    column = jnp.where(source < REACH, source - REACH, source - REACH + cx)
    weights = weight_of(column - lane)
    place[pl.ds(cx, SUB), :] = jnp.where(source < 2 * REACH, weights, 0.0)

    start = REACH * (1 - odd)
    together = math.gcd(slab, 16)

    def layers(s, _):
        spread = jnp.concatenate(
            [
                place[
                    pl.ds(
                        pl.multiple_of(
                            cx - GROUP * lax.rem(start + s * together + k, slab), SUB), cx), :
                ].astype(BF16)
                for k in range(together)
            ],
            axis=1,
        )
        columns = pl.ds(pl.multiple_of(s * together * cx, together * cx), together * cx)
        terms[:, columns] = jnp.dot(
            packed[...], jnp.concatenate([spread, spread], axis=0), preferred_element_type=F32
        )
        return 0

    lax.fori_loop(0, slab // together, layers, 0)

    def along(c, z, cell, rows, at):
        return stream[c, z, rows, :] + terms[at, cell * cx : (cell + 1) * cx]

    for k in range(REACH):
        cell = slab - REACH + k
        for c in range(3):
            stream_out[c, odd * (2 - 2 * k) + k, pl.ds(0, ny), :] = along(
                c, lax.rem(start + cell, slab), cell, slice(None), pl.ds(c * ny, ny))

    pairs = tables(colour_map)
    first_depth = lax.axis_index("depth") * slab + start

    def tile(t):
        rows = pl.ds(pl.multiple_of(t * SUB, SUB), SUB)
        count = counts[rows, :] - first_depth
        colour = [jnp.zeros((SUB, cx), F32) for _ in range(3)]
        clear = jnp.ones((SUB, cx), F32)
        for cell in range(slab - REACH):
            dx = [
                along(c, start + cell, cell, rows, pl.ds(pl.multiple_of(c * ny + t * SUB, SUB), SUB))
                for c in range(3)
            ]
            dy, dz, rest, turn = [span[k, start + cell, rows, :] for k in range(4)]
            square = rest + dx[0] * dx[0] + 2.0 * (dy * dx[1] + dz * dx[2])
            w1 = dz - dx[2]
            w2 = dx[1] - dy
            spin = turn + w1 * w1 + w2 * w2
            passed, values, strength = shade(square, spin, count > cell, pairs, total_depth)
            after = clear * passed
            weight = (clear - after) * strength
            colour = [colour[k] + weight * values[k] for k in range(3)]
            clear = after
        for k in range(3):
            part[k, rows, :] = colour[k] * (1.0 / UNIT)
        part[3, rows, :] = clear

    unroll = math.gcd(ny // SUB, 3)

    def tiles(s, _):
        for k in range(unroll):
            tile(s * unroll + k)
        return 0

    lax.fori_loop(0, ny // SUB // unroll, tiles, 0)


def outer_kernel(total_depth, own, far, outline, stream, part, counts, colour_map, out):
    chips, _, share, cx = out.shape
    odd = parity()
    me = lax.axis_index("depth")
    slab = total_depth // lax.axis_size("depth")
    pairs = tables(colour_map)
    sign = jnp.full((SUB, cx), 2 * odd - 1, jnp.int32).astype(F32)
    front = jnp.full((SUB, cx), odd, jnp.int32) == 0
    weights = [45.0 * sign, -9.0 * sign, sign]

    def window(rows):
        count = counts[rows, :] - me * slab
        beyond = [
            [far[c, (1 - odd) * (2 - 2 * r) + r, rows, :] for r in range(REACH)]
            for c in range(3)
        ]
        layers = []
        for q in range(REACH):
            dx = [stream[c, q, rows, :] for c in range(3)]
            dy = [outline[c, q, rows, :] for c in range(3)]
            dz = [outline[3 + c, q, rows, :] for c in range(3)]
            for c in range(3):
                for r in range(REACH - q):
                    dz[c] = dz[c] + weights[q + r] * beyond[c][r]
            w0 = dy[2] - dz[1]
            w1 = dz[0] - dx[2]
            w2 = dx[1] - dy[0]
            square = dx[0] * dx[0] + dy[1] * dy[1] + dz[2] * dz[2]
            square = square + 2.0 * (dy[0] * dx[1] + dz[0] * dx[2] + dz[1] * dy[2])
            spin = w0 * w0 + w1 * w1 + w2 * w2
            seen = count > odd * (slab - 1 - 2 * q) + q
            passed, values, strength = shade(square, spin, seen, pairs, total_depth)
            weight = (1.0 - passed) * (strength * (1.0 / UNIT))
            layers.append([weight * value for value in values] + [passed])
        first = [jnp.where(front, a, b) for a, b in zip(layers[0], layers[2])]
        last = [jnp.where(front, b, a) for a, b in zip(layers[0], layers[2])]
        clear = first[3] * layers[1][3]
        rest = part[3, rows, :]
        outer_clear = clear * last[3]
        image = []
        for k in range(3):
            edge = first[k] + first[3] * layers[1][k] + clear * last[k]
            inner = part[k, rows, :]
            image.append(jnp.where(front, edge + outer_clear * inner, inner + rest * edge))
        return image + [1.0 - outer_clear * rest]

    owner = odd if own else 1 - odd
    starts = sorted({min(w, max(share - SUB, 0)) for w in range(0, share, SUB)})
    height = min(share, SUB)
    for s in range(chips):
        chip = lax.rem(me // 2 + s, chips)
        for w in starts:
            row = (2 * chip + owner) * share + w
            image = window(pl.ds(row, SUB))
            for k in range(4):
                out[s, k, pl.ds(w, height), :] = image[k][:height]


def over(front, back):
    return front + (1.0 - front[..., 3:, :, :]) * back


def gather_rays(mine, theirs):
    chips = mine.shape[0]
    devices = 2 * chips
    me = lax.axis_index("depth")
    odd = lax.rem(me, 2) == 1
    theirs = lax.ppermute(theirs, "depth", [(i, i + 1 - 2 * (i % 2)) for i in range(devices)])
    both = over(jnp.where(odd, theirs, mine), jnp.where(odd, mine, theirs))
    got = [both[0]] + [
        lax.ppermute(both[s], "depth", [(i, (i + 2 * s) % devices) for i in range(devices)])
        for s in range(1, chips)
    ]
    half = chips // 2
    chip = me // 2
    pivot = lax.rem(chip - half + chips, chips)
    first = last = jnp.zeros_like(got[0])
    for k in range(1, chips):
        s = (half - k) % chips
        before = lax.rem(chip - s + chips, chips) < pivot
        first = over(first, jnp.where(before, got[s], 0.0))
        last = over(last, jnp.where(before, 0.0, got[s]))
    return over(over(first, got[half]), last)


def vmem(count):
    return [pl.BlockSpec(memory_space=pltpu.VMEM)] * count


def held(*dims):
    return pltpu.VMEM(dims, F32)


def in_vmem(x):
    return pltpu.with_memory_space_constraint(x, pltpu.VMEM)


def per_device(velocity, metric, colour_map, counts):
    _, slab, ny, cx = velocity.shape
    devices = lax.axis_size("depth")
    tiles = lax.axis_size("tile")
    total_depth = slab * devices
    scalars = pl.BlockSpec(memory_space=pltpu.SMEM)

    def limit(size):
        return pltpu.CompilerParams(vmem_limit_bytes=size * MIB)

    hbm = pl.BlockSpec(memory_space=pltpu.HBM)
    share = ny // devices
    spare = SUB if share < SUB else 0
    padded = (3, slab + 2 * REACH, ny + 2 * SUB, cx)
    columns = (3, ny // 2, cx)
    up = [(i, (i + 1) % devices) for i in range(devices)]
    down = [(i, (i - 1) % devices) for i in range(devices)]
    whole = pltpu.with_memory_space_constraint(velocity, pltpu.HBM)
    near, far = pl.pallas_call(
        ends_kernel,
        out_shape=(held(3, REACH, ny, cx), held(3, REACH, ny + spare, cx)),
        in_specs=[hbm],
        out_specs=tuple(vmem(2)),
        scratch_shapes=[pltpu.SemaphoreType.DMA((2,))],
        compiler_params=limit(4),
        name="ends",
    )(whole)
    near = lax.ppermute(near, "depth", [(down if i % 2 else up)[i] for i in range(devices)])
    far = lax.ppermute(far, "depth", [(up if i % 2 else down)[i] for i in range(devices)])

    ext, to_right, to_left = pl.pallas_call(
        edges_kernel,
        out_shape=(held(*padded), held(*columns), held(*columns)),
        in_specs=vmem(1),
        out_specs=tuple(vmem(3)),
        scratch_shapes=[pltpu.SemaphoreType.DMA((1,))],
        compiler_params=limit(4),
        name="edges",
    )(velocity)
    from_left = lax.ppermute(to_right, "tile", [(i, (i + 1) % tiles) for i in range(tiles)])
    from_right = lax.ppermute(to_left, "tile", [(i, (i - 1) % tiles) for i in range(tiles)])

    stream, span, outline = pl.pallas_call(
        slopes_kernel,
        out_shape=(
            held(3, slab, ny, cx),
            held(4, slab, ny, cx),
            held(6, REACH, ny + spare, cx),
        ),
        in_specs=vmem(2) + [scalars],
        out_specs=tuple(vmem(3)),
        scratch_shapes=[pltpu.VMEM((2 * cx, cx), BF16)],
        compiler_params=limit(4),
        name="slopes",
    )(in_vmem(ext), in_vmem(near), metric)

    part, stream = pl.pallas_call(
        functools.partial(inner_kernel, total_depth),
        out_shape=(held(4, ny + spare, cx), held(3, REACH, ny + spare, cx)),
        in_specs=vmem(6),
        out_specs=tuple(vmem(2)),
        scratch_shapes=[
            pltpu.VMEM((3 * ny, slab * cx), F32),
            pltpu.VMEM((3 * ny, 2 * cx), BF16),
            pltpu.VMEM((2 * cx, cx), F32),
        ],
        compiler_params=limit(8),
        name="inner",
    )(*map(in_vmem, (stream, span, from_left, from_right, counts, colour_map)))

    tall = jnp.pad(counts, ((0, spare), (0, 0))) if spare else counts
    rest = tuple(map(in_vmem, (far, outline, stream, part, tall, colour_map)))

    def outer(own, name):
        return pl.pallas_call(
            functools.partial(outer_kernel, total_depth, own),
            out_shape=held(devices // 2, 4, share, cx),
            in_specs=vmem(6),
            out_specs=vmem(1)[0],
            compiler_params=limit(4),
            name=name,
        )(*rest)

    theirs = outer(False, "theirs")
    return gather_rays(outer(True, "mine"), theirs)


def solution(mesh):
    in_specs = (P(None, "depth", None, "tile"), P(), P(), P(None, "tile"))
    out_specs = P(None, "depth", "tile")
    return jax.shard_map(
        per_device, mesh=mesh, in_specs=in_specs, out_specs=out_specs, check_vma=False
    )
```

```python
import functools
import math

import jax
import jax.numpy as jnp
from jax import lax
from jax.experimental import pallas as pl
from jax.experimental.pallas import tpu as pltpu
from jax.sharding import PartitionSpec as P

REACH = 3
SUB = 8
GROUP = 8
CRITERION_SCALE = 2.0
VORTEX_SCALE = 4.0
OPTICAL_DEPTH = 4.0
LOG2_E = 1.4426950408889634
TINY = 1.2e-38
FIELD = 13
UNIT = 4096.0
MIB = 1024 * 1024
F32 = jnp.float32
BF16 = jnp.bfloat16


def parity():
    return lax.rem(lax.axis_index("depth"), 2)


def stencil(ahead, behind):
    return 45.0 * (ahead[0] - behind[0]) - 9.0 * (ahead[1] - behind[1]) + (ahead[2] - behind[2])


def weight_of(distance):
    out = jnp.zeros(distance.shape, F32)
    for k, weight in ((1, 45.0), (2, -9.0), (3, 1.0)):
        out = jnp.where(distance == k, weight, out)
        out = jnp.where(distance == -k, -weight, out)
    return out


def halves(x):
    high = x.astype(BF16)
    low = (x - high.astype(F32)).astype(BF16)
    return jnp.concatenate([high, low], axis=1)


def ends_kernel(vel, near, far, sems):
    odd = parity()
    last = vel.shape[1] - REACH
    rows = pl.ds(0, vel.shape[2])
    copies = [
        pltpu.make_async_copy(
            vel.at[:, pl.ds(odd * last, REACH)], far.at[:, :, rows, :], sems.at[0]),
        pltpu.make_async_copy(vel.at[:, pl.ds((1 - odd) * last, REACH)], near, sems.at[1]),
    ]
    for copy in copies:
        copy.start()
    for copy in copies:
        copy.wait()


def edges_kernel(vel, ext, right_out, left_out, sem):
    slab, ny, cx = vel.shape[1:]
    half = ny // 2
    body = pl.ds(SUB, ny)
    copy = pltpu.make_async_copy(vel, ext.at[:, pl.ds(REACH, slab), body, :], sem.at[0])
    copy.start()
    zero = jnp.zeros((SUB, cx), F32)
    for c in range(3):
        for z in range(slab):
            ext[c, REACH + z, pl.ds(0, SUB), :] = zero
            ext[c, REACH + z, pl.ds(ny + SUB, SUB), :] = zero
        for z in range(REACH):
            ext[c, z, body, :] = jnp.zeros((ny, cx), F32)
            ext[c, REACH + slab + z, body, :] = jnp.zeros((ny, cx), F32)
    lane = lax.broadcasted_iota(jnp.int32, (SUB, cx), 1)

    def tile(t, _):
        for c in range(3):
            to_right = jnp.zeros((SUB, cx), F32)
            to_left = jnp.zeros((SUB, cx), F32)
            for z in range(slab):
                for h in range(2):
                    first = GROUP * z + 4 * h
                    rows = pl.ds(pl.multiple_of(h * half + t * SUB, SUB), SUB)
                    turned = pltpu.roll(vel[c, z, rows, :], (first + REACH) % cx, 1)
                    to_right = jnp.where((lane >= first) & (lane < first + 4), turned, to_right)
                    place = lax.rem(lane + (2 * cx - first - REACH), cx)
                    to_left = jnp.where(place < 4, turned, to_left)
            rows = pl.ds(pl.multiple_of(t * SUB, SUB), SUB)
            right_out[c, rows, :] = to_right
            left_out[c, rows, :] = to_left
        return 0

    lax.fori_loop(0, half // SUB, tile, 0)
    copy.wait()


def slopes_kernel(ext, near, metric, stream, span, outline, band):
    slab, ny, cx = stream.shape[1:]
    odd = parity()
    body = pl.ds(SUB, ny)
    source = lax.broadcasted_iota(jnp.int32, (cx, cx), 0)
    target = lax.broadcasted_iota(jnp.int32, (cx, cx), 1)
    weights = weight_of(source - target).astype(BF16)
    band[pl.ds(0, cx), :] = weights
    band[pl.ds(cx, cx), :] = weights
    row = lax.broadcasted_iota(jnp.int32, (SUB, cx), 0)
    sign = jnp.full((SUB, cx), 1 - 2 * odd, jnp.int32).astype(F32)
    reach = [45.0 * sign, -9.0 * sign, sign]
    steps = math.gcd(slab, ny // SUB)
    layers = slab // steps
    tiles = ny // SUB // steps

    def along(z):
        rows = jnp.concatenate([halves(ext[c, REACH + z, body, :]) for c in range(3)], axis=0)
        out = jnp.dot(rows, band[...], preferred_element_type=F32)
        for c in range(3):
            stream[c, z] = out[c * ny : (c + 1) * ny]

    def tile(t):
        base = pl.multiple_of(t * SUB, SUB)
        rows = pl.ds(base, SUB)
        inner = pl.ds(base + SUB, SUB)
        scale = jnp.zeros((SUB, cx), F32)
        for r in range(SUB):
            scale = jnp.where(row == r, metric[base + r], scale)

        def slopes(z):
            dy = [
                scale * stencil(
                    [ext[c, REACH + z, pl.ds(base + SUB + k, SUB), :] for k in (1, 2, 3)],
                    [ext[c, REACH + z, pl.ds(base + SUB - k, SUB), :] for k in (1, 2, 3)],
                )
                for c in range(3)
            ]
            dz = [
                stencil(
                    [ext[c, REACH + z + k, inner, :] for k in (1, 2, 3)],
                    [ext[c, REACH + z - k, inner, :] for k in (1, 2, 3)],
                )
                for c in range(3)
            ]
            return dy, dz

        def keep(z, dy, dz):
            turn = dy[2] - dz[1]
            span[0, z, rows, :] = dy[0]
            span[1, z, rows, :] = dz[0]
            span[2, z, rows, :] = dy[1] * dy[1] + dz[2] * dz[2] + 2.0 * (dy[2] * dz[1])
            span[3, z, rows, :] = turn * turn

        for z in range(REACH, slab - REACH):
            keep(z, *slopes(z))
        beyond = [[near[c, odd * (2 - 2 * r) + r, rows, :] for r in range(REACH)] for c in range(3)]
        for q in range(REACH):
            low, high = q, slab - 1 - q
            z = odd * (low - high) + high
            dy, dz = slopes(z)
            for c in range(3):
                for r in range(REACH - q):
                    dz[c] = dz[c] + reach[q + r] * beyond[c][r]
            keep(z, dy, dz)
            dy, dz = slopes(odd * (high - low) + low)
            for c in range(3):
                outline[c, q, rows, :] = dy[c]
                outline[3 + c, q, rows, :] = dz[c]

    def step(s, _):
        for k in range(layers):
            along(s * layers + k)
        for k in range(tiles):
            tile(s * tiles + k)
        return 0

    lax.fori_loop(0, steps, step, 0)


def tables(colour_map):
    bins = colour_map.shape[1]
    table = colour_map[...].astype(F32) * UNIT
    after = pltpu.roll(table, bins - 1, 1)
    packed = table.astype(jnp.int32) * (1 << FIELD) + after.astype(jnp.int32)
    return [jnp.broadcast_to(packed[k : k + 1], (SUB, bins)) for k in range(4)]


def shade(square, spin, seen, pairs, total_depth):
    bins = pairs[0].shape[1]
    half_top = (bins - 1) * 0.5
    level = half_top + half_top * jnp.tanh(square * (-0.5 / (3600.0 * CRITERION_SCALE)))
    low = jnp.minimum(jnp.floor(level), bins - 2.0)
    fraction = level - low
    index = low.astype(jnp.int32)

    def value(k):
        pair = jnp.take_along_axis(pairs[k], index, axis=1)
        first = lax.shift_right_logical(pair, FIELD).astype(F32)
        second = (pair & ((1 << FIELD) - 1)).astype(F32)
        return first + fraction * (second - first)

    gain = -LOG2_E * OPTICAL_DEPTH / (total_depth * UNIT)
    passed = jnp.exp2(jnp.where(seen, value(0) * gain, 0.0))
    length = spin * lax.rsqrt(jnp.maximum(spin, TINY))
    strength = jnp.tanh(length * (1.0 / (60.0 * VORTEX_SCALE)))
    return passed, [value(k) for k in (1, 2, 3)], strength


def inner_kernel(
    total_depth, stream, span, from_left, from_right, counts, colour_map,
    part, stream_out, terms, packed, place,
):
    slab, ny, cx = stream.shape[1:]
    half = ny // 2
    odd = parity()
    lane = lax.broadcasted_iota(jnp.int32, (SUB, cx), 1)
    within = lax.rem(lane, GROUP)

    def pack(t, _):
        rows = pl.ds(pl.multiple_of(2 * t * SUB, 2 * SUB), 2 * SUB)
        wide = lax.rem(lax.broadcasted_iota(jnp.int32, (2 * SUB, cx), 1), GROUP)
        for c in range(3):
            right = from_left[c, rows, :]
            left = from_right[c, rows, :]
            first = jnp.where(wide < 3, right, left)
            second = pltpu.roll(jnp.where((wide >= 4) & (wide < 7), right, left), cx - 4, 1)
            at = pl.multiple_of(c * ny + 2 * t * SUB, 2 * SUB)
            packed[pl.ds(at, 2 * SUB), :] = halves(first)
            packed[pl.ds(pl.multiple_of(at + half, 2 * SUB), 2 * SUB), :] = halves(second)
        return 0

    lax.fori_loop(0, half // (2 * SUB), pack, 0)
    place[...] = jnp.zeros(place.shape, F32)
    source = lax.broadcasted_iota(jnp.int32, (SUB, cx), 0)
    column = jnp.where(source < REACH, source - REACH, source - REACH + cx)
    weights = weight_of(column - lane)
    place[pl.ds(cx, SUB), :] = jnp.where(source < 2 * REACH, weights, 0.0)

    start = REACH * (1 - odd)
    together = math.gcd(slab, 16)

    def layers(s, _):
        spread = jnp.concatenate(
            [
                place[
                    pl.ds(
                        pl.multiple_of(
                            cx - GROUP * lax.rem(start + s * together + k, slab), SUB), cx), :
                ].astype(BF16)
                for k in range(together)
            ],
            axis=1,
        )
        columns = pl.ds(pl.multiple_of(s * together * cx, together * cx), together * cx)
        terms[:, columns] = jnp.dot(
            packed[...], jnp.concatenate([spread, spread], axis=0), preferred_element_type=F32
        )
        return 0

    lax.fori_loop(0, slab // together, layers, 0)

    def along(c, z, cell, rows, at):
        return stream[c, z, rows, :] + terms[at, cell * cx : (cell + 1) * cx]

    for k in range(REACH):
        cell = slab - REACH + k
        for c in range(3):
            stream_out[c, odd * (2 - 2 * k) + k, pl.ds(0, ny), :] = along(
                c, lax.rem(start + cell, slab), cell, slice(None), pl.ds(c * ny, ny))

    pairs = tables(colour_map)
    first_depth = lax.axis_index("depth") * slab + start

    def tile(t):
        rows = pl.ds(pl.multiple_of(t * SUB, SUB), SUB)
        count = counts[rows, :] - first_depth
        colour = [jnp.zeros((SUB, cx), F32) for _ in range(3)]
        clear = jnp.ones((SUB, cx), F32)
        for cell in range(slab - REACH):
            dx = [
                along(c, start + cell, cell, rows, pl.ds(pl.multiple_of(c * ny + t * SUB, SUB), SUB))
                for c in range(3)
            ]
            dy, dz, rest, turn = [span[k, start + cell, rows, :] for k in range(4)]
            square = rest + dx[0] * dx[0] + 2.0 * (dy * dx[1] + dz * dx[2])
            w1 = dz - dx[2]
            w2 = dx[1] - dy
            spin = turn + w1 * w1 + w2 * w2
            passed, values, strength = shade(square, spin, count > cell, pairs, total_depth)
            after = clear * passed
            weight = (clear - after) * strength
            colour = [colour[k] + weight * values[k] for k in range(3)]
            clear = after
        for k in range(3):
            part[k, rows, :] = colour[k] * (1.0 / UNIT)
        part[3, rows, :] = clear

    unroll = math.gcd(ny // SUB, 3)

    def tiles(s, _):
        for k in range(unroll):
            tile(s * unroll + k)
        return 0

    lax.fori_loop(0, ny // SUB // unroll, tiles, 0)


def owner_chip(chip, k, chips):
    return chip ^ k if chips in (2, 4) else lax.rem(chip + k, chips)


def outer_kernel(total_depth, own, far, outline, stream, part, counts, colour_map, out):
    chips, _, share, cx = out.shape
    odd = parity()
    me = lax.axis_index("depth")
    slab = total_depth // lax.axis_size("depth")
    pairs = tables(colour_map)
    sign = jnp.full((SUB, cx), 2 * odd - 1, jnp.int32).astype(F32)
    front = jnp.full((SUB, cx), odd, jnp.int32) == 0
    weights = [45.0 * sign, -9.0 * sign, sign]

    def window(rows):
        count = counts[rows, :] - me * slab
        beyond = [
            [far[c, (1 - odd) * (2 - 2 * r) + r, rows, :] for r in range(REACH)]
            for c in range(3)
        ]
        layers = []
        for q in range(REACH):
            dx = [stream[c, q, rows, :] for c in range(3)]
            dy = [outline[c, q, rows, :] for c in range(3)]
            dz = [outline[3 + c, q, rows, :] for c in range(3)]
            for c in range(3):
                for r in range(REACH - q):
                    dz[c] = dz[c] + weights[q + r] * beyond[c][r]
            w0 = dy[2] - dz[1]
            w1 = dz[0] - dx[2]
            w2 = dx[1] - dy[0]
            square = dx[0] * dx[0] + dy[1] * dy[1] + dz[2] * dz[2]
            square = square + 2.0 * (dy[0] * dx[1] + dz[0] * dx[2] + dz[1] * dy[2])
            spin = w0 * w0 + w1 * w1 + w2 * w2
            seen = count > odd * (slab - 1 - 2 * q) + q
            passed, values, strength = shade(square, spin, seen, pairs, total_depth)
            weight = (1.0 - passed) * (strength * (1.0 / UNIT))
            layers.append([weight * value for value in values] + [passed])
        first = [jnp.where(front, a, b) for a, b in zip(layers[0], layers[2])]
        last = [jnp.where(front, b, a) for a, b in zip(layers[0], layers[2])]
        clear = first[3] * layers[1][3]
        rest = part[3, rows, :]
        outer_clear = clear * last[3]
        image = []
        for k in range(3):
            edge = first[k] + first[3] * layers[1][k] + clear * last[k]
            inner = part[k, rows, :]
            image.append(jnp.where(front, edge + outer_clear * inner, inner + rest * edge))
        return image + [1.0 - outer_clear * rest]

    owner = odd if own else 1 - odd
    starts = sorted({min(w, max(share - SUB, 0)) for w in range(0, share, SUB)})
    height = min(share, SUB)
    for s in range(chips):
        chip = owner_chip(me // 2, s, chips)
        for w in starts:
            row = (2 * chip + owner) * share + w
            image = window(pl.ds(row, SUB))
            for k in range(4):
                out[s, k, pl.ds(w, height), :] = image[k][:height]


def over(front, back):
    return front + (1.0 - front[..., 3:, :, :]) * back


def gather_rays(mine, theirs):
    chips = mine.shape[0]
    devices = 2 * chips
    me = lax.axis_index("depth")
    odd = lax.rem(me, 2) == 1
    theirs = lax.ppermute(theirs, "depth", [(i, i + 1 - 2 * (i % 2)) for i in range(devices)])
    both = over(jnp.where(odd, theirs, mine), jnp.where(odd, mine, theirs))
    chip = me // 2
    if chips in (2, 4):
        step, source = (1, 2, 3), lambda k: chip ^ k
        rings = {k: [(i, i ^ (2 * k)) for i in range(devices)] for k in range(1, chips)}
    else:
        step, source = range(1, chips), lambda k: lax.rem(chip - k + chips, chips)
        rings = {k: [(i, (i + 2 * k) % devices) for i in range(devices)] for k in range(1, chips)}
    order = [0] + [k for k in step if k < chips]
    got = [both[0]] + [lax.ppermute(both[k], "depth", rings[k]) for k in order[1:]]
    chip_of = [source(k) for k in order]
    weights, image = [], 0.0
    for n, layer in enumerate(got):
        clear = 1.0 - layer[3:]
        weights = [
            w * jnp.where(chip_of[n] < chip_of[m], clear, 1.0) for m, w in enumerate(weights)
        ]
        own = jnp.ones_like(clear)
        for m in range(n):
            own = own * jnp.where(chip_of[m] < chip_of[n], 1.0 - got[m][3:], 1.0)
        weights.append(own)
    return sum(w * layer for w, layer in zip(weights, got))


def vmem(count):
    return [pl.BlockSpec(memory_space=pltpu.VMEM)] * count


def held(*dims):
    return pltpu.VMEM(dims, F32)


def in_vmem(x):
    return pltpu.with_memory_space_constraint(x, pltpu.VMEM)


def per_device(velocity, metric, colour_map, counts):
    _, slab, ny, cx = velocity.shape
    devices = lax.axis_size("depth")
    tiles = lax.axis_size("tile")
    total_depth = slab * devices
    scalars = pl.BlockSpec(memory_space=pltpu.SMEM)

    def limit(size):
        return pltpu.CompilerParams(vmem_limit_bytes=size * MIB)

    hbm = pl.BlockSpec(memory_space=pltpu.HBM)
    share = ny // devices
    spare = SUB if share < SUB else 0
    padded = (3, slab + 2 * REACH, ny + 2 * SUB, cx)
    columns = (3, ny // 2, cx)
    up = [(i, (i + 1) % devices) for i in range(devices)]
    down = [(i, (i - 1) % devices) for i in range(devices)]
    whole = pltpu.with_memory_space_constraint(velocity, pltpu.HBM)
    near, far = pl.pallas_call(
        ends_kernel,
        out_shape=(held(3, REACH, ny, cx), held(3, REACH, ny + spare, cx)),
        in_specs=[hbm],
        out_specs=tuple(vmem(2)),
        scratch_shapes=[pltpu.SemaphoreType.DMA((2,))],
        compiler_params=limit(4),
        name="ends",
    )(whole)
    near = lax.ppermute(near, "depth", [(down if i % 2 else up)[i] for i in range(devices)])
    far = lax.ppermute(far, "depth", [(up if i % 2 else down)[i] for i in range(devices)])

    ext, to_right, to_left = pl.pallas_call(
        edges_kernel,
        out_shape=(held(*padded), held(*columns), held(*columns)),
        in_specs=vmem(1),
        out_specs=tuple(vmem(3)),
        scratch_shapes=[pltpu.SemaphoreType.DMA((1,))],
        compiler_params=limit(4),
        name="edges",
    )(velocity)
    from_left = lax.ppermute(to_right, "tile", [(i, (i + 1) % tiles) for i in range(tiles)])
    from_right = lax.ppermute(to_left, "tile", [(i, (i - 1) % tiles) for i in range(tiles)])

    stream, span, outline = pl.pallas_call(
        slopes_kernel,
        out_shape=(
            held(3, slab, ny, cx),
            held(4, slab, ny, cx),
            held(6, REACH, ny + spare, cx),
        ),
        in_specs=vmem(2) + [scalars],
        out_specs=tuple(vmem(3)),
        scratch_shapes=[pltpu.VMEM((2 * cx, cx), BF16)],
        compiler_params=limit(4),
        name="slopes",
    )(in_vmem(ext), in_vmem(near), metric)

    part, stream = pl.pallas_call(
        functools.partial(inner_kernel, total_depth),
        out_shape=(held(4, ny + spare, cx), held(3, REACH, ny + spare, cx)),
        in_specs=vmem(6),
        out_specs=tuple(vmem(2)),
        scratch_shapes=[
            pltpu.VMEM((3 * ny, slab * cx), F32),
            pltpu.VMEM((3 * ny, 2 * cx), BF16),
            pltpu.VMEM((2 * cx, cx), F32),
        ],
        compiler_params=limit(8),
        name="inner",
    )(*map(in_vmem, (stream, span, from_left, from_right, counts, colour_map)))

    tall = jnp.pad(counts, ((0, spare), (0, 0))) if spare else counts
    rest = tuple(map(in_vmem, (far, outline, stream, part, tall, colour_map)))

    def outer(own, name):
        return pl.pallas_call(
            functools.partial(outer_kernel, total_depth, own),
            out_shape=held(devices // 2, 4, share, cx),
            in_specs=vmem(6),
            out_specs=vmem(1)[0],
            compiler_params=limit(4),
            name=name,
        )(*rest)

    theirs = outer(False, "theirs")
    return gather_rays(outer(True, "mine"), theirs)


def solution(mesh):
    in_specs = (P(None, "depth", None, "tile"), P(), P(), P(None, "tile"))
    out_specs = P(None, "depth", "tile")
    return jax.shard_map(
        per_device, mesh=mesh, in_specs=in_specs, out_specs=out_specs, check_vma=False
    )
```

```python
import functools
import math

import jax
import jax.numpy as jnp
from jax import lax
from jax.experimental import pallas as pl
from jax.experimental.pallas import tpu as pltpu
from jax.sharding import PartitionSpec as P

REACH = 3
SUB = 8
GROUP = 8
CRITERION_SCALE = 2.0
VORTEX_SCALE = 4.0
OPTICAL_DEPTH = 4.0
LOG2_E = 1.4426950408889634
TINY = 1.2e-38
FIELD = 13
UNIT = 4096.0
MIB = 1024 * 1024
F32 = jnp.float32
BF16 = jnp.bfloat16


def parity():
    return lax.rem(lax.axis_index("depth"), 2)


def stencil(ahead, behind):
    return 45.0 * (ahead[0] - behind[0]) - 9.0 * (ahead[1] - behind[1]) + (ahead[2] - behind[2])


def weight_of(distance):
    out = jnp.zeros(distance.shape, F32)
    for k, weight in ((1, 45.0), (2, -9.0), (3, 1.0)):
        out = jnp.where(distance == k, weight, out)
        out = jnp.where(distance == -k, -weight, out)
    return out


def halves(x):
    high = x.astype(BF16)
    low = (x - high.astype(F32)).astype(BF16)
    return jnp.concatenate([high, low], axis=1)


def ends_kernel(vel, near, far, sems):
    odd = parity()
    last = vel.shape[1] - REACH
    rows = pl.ds(0, vel.shape[2])
    copies = [
        pltpu.make_async_copy(
            vel.at[:, pl.ds(odd * last, REACH)], far.at[:, :, rows, :], sems.at[0]),
        pltpu.make_async_copy(vel.at[:, pl.ds((1 - odd) * last, REACH)], near, sems.at[1]),
    ]
    for copy in copies:
        copy.start()
    for copy in copies:
        copy.wait()


def edges_kernel(vel, ext, right_out, left_out, sem):
    slab, ny, cx = vel.shape[1:]
    half = ny // 2
    body = pl.ds(SUB, ny)
    copy = pltpu.make_async_copy(vel, ext.at[:, pl.ds(REACH, slab), body, :], sem.at[0])
    copy.start()
    zero = jnp.zeros((SUB, cx), F32)
    steps = half // SUB
    layers = -(-slab // steps)
    lane = lax.broadcasted_iota(jnp.int32, (SUB, cx), 1)

    def tile(t, _):
        for c in range(3):
            for k in range(layers):
                z = REACH + jnp.minimum(t * layers + k, slab - 1)
                ext[c, z, pl.ds(0, SUB), :] = zero
                ext[c, z, pl.ds(ny + SUB, SUB), :] = zero
            for z in range(REACH):
                for h in range(2):
                    rows = pl.ds(pl.multiple_of(SUB + h * half + t * SUB, SUB), SUB)
                    ext[c, z, rows, :] = zero
                    ext[c, REACH + slab + z, rows, :] = zero
            to_right = jnp.zeros((SUB, cx), F32)
            to_left = jnp.zeros((SUB, cx), F32)
            for z in range(slab):
                for h in range(2):
                    first = GROUP * z + 4 * h
                    rows = pl.ds(pl.multiple_of(h * half + t * SUB, SUB), SUB)
                    turned = pltpu.roll(vel[c, z, rows, :], (first + REACH) % cx, 1)
                    to_right = jnp.where((lane >= first) & (lane < first + 4), turned, to_right)
                    place = lax.rem(lane + (2 * cx - first - REACH), cx)
                    to_left = jnp.where(place < 4, turned, to_left)
            rows = pl.ds(pl.multiple_of(t * SUB, SUB), SUB)
            right_out[c, rows, :] = to_right
            left_out[c, rows, :] = to_left
        return 0

    lax.fori_loop(0, half // SUB, tile, 0)
    copy.wait()


def slopes_kernel(ext, near, metric, stream, span, outline, band):
    slab, ny, cx = stream.shape[1:]
    odd = parity()
    body = pl.ds(SUB, ny)
    source = lax.broadcasted_iota(jnp.int32, (cx, cx), 0)
    target = lax.broadcasted_iota(jnp.int32, (cx, cx), 1)
    weights = weight_of(source - target).astype(BF16)
    band[pl.ds(0, cx), :] = weights
    band[pl.ds(cx, cx), :] = weights
    row = lax.broadcasted_iota(jnp.int32, (SUB, cx), 0)
    sign = jnp.full((SUB, cx), 1 - 2 * odd, jnp.int32).astype(F32)
    reach = [45.0 * sign, -9.0 * sign, sign]
    steps = math.gcd(slab, ny // SUB)
    layers = slab // steps
    tiles = ny // SUB // steps

    def along(z):
        rows = jnp.concatenate([halves(ext[c, REACH + z, body, :]) for c in range(3)], axis=0)
        out = jnp.dot(rows, band[...], preferred_element_type=F32)
        for c in range(3):
            stream[c, z] = out[c * ny : (c + 1) * ny]

    def tile(t):
        base = pl.multiple_of(t * SUB, SUB)
        rows = pl.ds(base, SUB)
        inner = pl.ds(base + SUB, SUB)
        scale = jnp.zeros((SUB, cx), F32)
        for r in range(SUB):
            scale = jnp.where(row == r, metric[base + r], scale)

        def slopes(z):
            dy = [
                scale * stencil(
                    [ext[c, REACH + z, pl.ds(base + SUB + k, SUB), :] for k in (1, 2, 3)],
                    [ext[c, REACH + z, pl.ds(base + SUB - k, SUB), :] for k in (1, 2, 3)],
                )
                for c in range(3)
            ]
            dz = [
                stencil(
                    [ext[c, REACH + z + k, inner, :] for k in (1, 2, 3)],
                    [ext[c, REACH + z - k, inner, :] for k in (1, 2, 3)],
                )
                for c in range(3)
            ]
            return dy, dz

        def keep(z, dy, dz):
            turn = dy[2] - dz[1]
            span[0, z, rows, :] = dy[0]
            span[1, z, rows, :] = dz[0]
            span[2, z, rows, :] = dy[1] * dy[1] + dz[2] * dz[2] + 2.0 * (dy[2] * dz[1])
            span[3, z, rows, :] = turn * turn

        for z in range(REACH, slab - REACH):
            keep(z, *slopes(z))
        beyond = [[near[c, odd * (2 - 2 * r) + r, rows, :] for r in range(REACH)] for c in range(3)]
        for q in range(REACH):
            low, high = q, slab - 1 - q
            z = odd * (low - high) + high
            dy, dz = slopes(z)
            for c in range(3):
                for r in range(REACH - q):
                    dz[c] = dz[c] + reach[q + r] * beyond[c][r]
            keep(z, dy, dz)
            dy, dz = slopes(odd * (high - low) + low)
            for c in range(3):
                outline[c, q, rows, :] = dy[c]
                outline[3 + c, q, rows, :] = dz[c]

    def step(s, _):
        for k in range(layers):
            along(s * layers + k)
        for k in range(tiles):
            tile(s * tiles + k)
        return 0

    lax.fori_loop(0, steps, step, 0)


def tables(colour_map):
    bins = colour_map.shape[1]
    table = colour_map[...].astype(F32) * UNIT
    after = pltpu.roll(table, bins - 1, 1)
    packed = table.astype(jnp.int32) * (1 << FIELD) + after.astype(jnp.int32)
    return [jnp.broadcast_to(packed[k : k + 1], (SUB, bins)) for k in range(4)]


def shade(square, spin, seen, pairs, total_depth):
    bins = pairs[0].shape[1]
    half_top = (bins - 1) * 0.5
    level = half_top + half_top * jnp.tanh(square * (-0.5 / (3600.0 * CRITERION_SCALE)))
    low = jnp.minimum(jnp.floor(level), bins - 2.0)
    fraction = level - low
    index = low.astype(jnp.int32)

    def value(k):
        pair = jnp.take_along_axis(pairs[k], index, axis=1, mode="promise_in_bounds")
        first = lax.shift_right_logical(pair, FIELD).astype(F32)
        second = (pair & ((1 << FIELD) - 1)).astype(F32)
        return first + fraction * (second - first)

    gain = -LOG2_E * OPTICAL_DEPTH / (total_depth * UNIT)
    passed = jnp.exp2(jnp.where(seen, value(0) * gain, 0.0))
    length = spin * lax.rsqrt(jnp.maximum(spin, TINY))
    strength = jnp.tanh(length * (1.0 / (60.0 * VORTEX_SCALE)))
    return passed, [value(k) for k in (1, 2, 3)], strength


def inner_kernel(
    total_depth, stream, span, from_left, from_right, counts, colour_map,
    part, stream_out, terms, packed, place,
):
    slab, ny, cx = stream.shape[1:]
    half = ny // 2
    odd = parity()
    lane = lax.broadcasted_iota(jnp.int32, (SUB, cx), 1)
    within = lax.rem(lane, GROUP)

    def pack(t, _):
        rows = pl.ds(pl.multiple_of(2 * t * SUB, 2 * SUB), 2 * SUB)
        wide = lax.rem(lax.broadcasted_iota(jnp.int32, (2 * SUB, cx), 1), GROUP)
        for c in range(3):
            right = from_left[c, rows, :]
            left = from_right[c, rows, :]
            first = jnp.where(wide < 3, right, left)
            second = pltpu.roll(jnp.where((wide >= 4) & (wide < 7), right, left), cx - 4, 1)
            at = pl.multiple_of(c * ny + 2 * t * SUB, 2 * SUB)
            packed[pl.ds(at, 2 * SUB), :] = halves(first)
            packed[pl.ds(pl.multiple_of(at + half, 2 * SUB), 2 * SUB), :] = halves(second)
        return 0

    lax.fori_loop(0, half // (2 * SUB), pack, 0)
    place[...] = jnp.zeros(place.shape, F32)
    source = lax.broadcasted_iota(jnp.int32, (SUB, cx), 0)
    column = jnp.where(source < REACH, source - REACH, source - REACH + cx)
    weights = weight_of(column - lane)
    place[pl.ds(cx, SUB), :] = jnp.where(source < 2 * REACH, weights, 0.0)

    start = REACH * (1 - odd)
    together = math.gcd(slab, 16)

    def layers(s, _):
        spread = jnp.concatenate(
            [
                place[
                    pl.ds(
                        pl.multiple_of(
                            cx - GROUP * lax.rem(start + s * together + k, slab), SUB), cx), :
                ].astype(BF16)
                for k in range(together)
            ],
            axis=1,
        )
        columns = pl.ds(pl.multiple_of(s * together * cx, together * cx), together * cx)
        terms[:, columns] = jnp.dot(
            packed[...], jnp.concatenate([spread, spread], axis=0), preferred_element_type=F32
        )
        return 0

    lax.fori_loop(0, slab // together, layers, 0)

    def along(c, z, cell, rows, at):
        return stream[c, z, rows, :] + terms[at, cell * cx : (cell + 1) * cx]

    for k in range(REACH):
        cell = slab - REACH + k
        for c in range(3):
            stream_out[c, odd * (2 - 2 * k) + k, pl.ds(0, ny), :] = along(
                c, lax.rem(start + cell, slab), cell, slice(None), pl.ds(c * ny, ny))

    pairs = tables(colour_map)
    first_depth = lax.axis_index("depth") * slab + start

    def tile(t):
        rows = pl.ds(pl.multiple_of(t * SUB, SUB), SUB)
        count = counts[rows, :] - first_depth
        colour = [jnp.zeros((SUB, cx), F32) for _ in range(3)]
        clear = jnp.ones((SUB, cx), F32)
        for cell in range(slab - REACH):
            dx = [
                along(c, start + cell, cell, rows, pl.ds(pl.multiple_of(c * ny + t * SUB, SUB), SUB))
                for c in range(3)
            ]
            dy, dz, rest, turn = [span[k, start + cell, rows, :] for k in range(4)]
            square = rest + dx[0] * dx[0] + 2.0 * (dy * dx[1] + dz * dx[2])
            w1 = dz - dx[2]
            w2 = dx[1] - dy
            spin = turn + w1 * w1 + w2 * w2
            passed, values, strength = shade(square, spin, count > cell, pairs, total_depth)
            after = clear * passed
            weight = (clear - after) * strength
            colour = [colour[k] + weight * values[k] for k in range(3)]
            clear = after
        for k in range(3):
            part[k, rows, :] = colour[k] * (1.0 / UNIT)
        part[3, rows, :] = clear

    unroll = math.gcd(ny // SUB, 12)

    def tiles(s, _):
        for k in range(unroll):
            tile(s * unroll + k)
        return 0

    lax.fori_loop(0, ny // SUB // unroll, tiles, 0)


def owner_chip(chip, k, chips):
    return chip ^ k if chips in (2, 4) else lax.rem(chip + k, chips)


def outer_kernel(total_depth, own, far, outline, stream, part, counts, colour_map, out):
    chips, _, share, cx = out.shape
    odd = parity()
    me = lax.axis_index("depth")
    slab = total_depth // lax.axis_size("depth")
    pairs = tables(colour_map)
    sign = jnp.full((SUB, cx), 2 * odd - 1, jnp.int32).astype(F32)
    front = jnp.full((SUB, cx), odd, jnp.int32) == 0
    weights = [45.0 * sign, -9.0 * sign, sign]

    def window(rows):
        count = counts[rows, :] - me * slab
        beyond = [
            [far[c, (1 - odd) * (2 - 2 * r) + r, rows, :] for r in range(REACH)]
            for c in range(3)
        ]
        layers = []
        for q in range(REACH):
            dx = [stream[c, q, rows, :] for c in range(3)]
            dy = [outline[c, q, rows, :] for c in range(3)]
            dz = [outline[3 + c, q, rows, :] for c in range(3)]
            for c in range(3):
                for r in range(REACH - q):
                    dz[c] = dz[c] + weights[q + r] * beyond[c][r]
            w0 = dy[2] - dz[1]
            w1 = dz[0] - dx[2]
            w2 = dx[1] - dy[0]
            square = dx[0] * dx[0] + dy[1] * dy[1] + dz[2] * dz[2]
            square = square + 2.0 * (dy[0] * dx[1] + dz[0] * dx[2] + dz[1] * dy[2])
            spin = w0 * w0 + w1 * w1 + w2 * w2
            seen = count > odd * (slab - 1 - 2 * q) + q
            passed, values, strength = shade(square, spin, seen, pairs, total_depth)
            weight = (1.0 - passed) * (strength * (1.0 / UNIT))
            layers.append([weight * value for value in values] + [passed])
        first = [jnp.where(front, a, b) for a, b in zip(layers[0], layers[2])]
        last = [jnp.where(front, b, a) for a, b in zip(layers[0], layers[2])]
        clear = first[3] * layers[1][3]
        rest = part[3, rows, :]
        outer_clear = clear * last[3]
        image = []
        for k in range(3):
            edge = first[k] + first[3] * layers[1][k] + clear * last[k]
            inner = part[k, rows, :]
            image.append(jnp.where(front, edge + outer_clear * inner, inner + rest * edge))
        return image + [1.0 - outer_clear * rest]

    owner = odd if own else 1 - odd
    starts = sorted({min(w, max(share - SUB, 0)) for w in range(0, share, SUB)})
    height = min(share, SUB)
    for s in range(chips):
        chip = owner_chip(me // 2, s, chips)
        for w in starts:
            row = (2 * chip + owner) * share + w
            image = window(pl.ds(row, SUB))
            for k in range(4):
                out[s, k, pl.ds(w, height), :] = image[k][:height]


def over(front, back):
    return front + (1.0 - front[..., 3:, :, :]) * back


def gather_rays(mine, theirs):
    chips = mine.shape[0]
    devices = 2 * chips
    me = lax.axis_index("depth")
    odd = lax.rem(me, 2) == 1
    theirs = lax.ppermute(theirs, "depth", [(i, i + 1 - 2 * (i % 2)) for i in range(devices)])
    both = over(jnp.where(odd, theirs, mine), jnp.where(odd, mine, theirs))
    chip = me // 2
    if chips in (2, 4):
        step, source = (2, 1, 3), lambda k: chip ^ k
        rings = {k: [(i, i ^ (2 * k)) for i in range(devices)] for k in range(1, chips)}
    else:
        step, source = range(1, chips), lambda k: lax.rem(chip - k + chips, chips)
        rings = {k: [(i, (i + 2 * k) % devices) for i in range(devices)] for k in range(1, chips)}
    order = [0] + [k for k in step if k < chips]
    got = [both[0]] + [lax.ppermute(both[k], "depth", rings[k]) for k in order[1:]]
    chip_of = [source(k) for k in order]
    weights, image = [], 0.0
    for n, layer in enumerate(got):
        clear = 1.0 - layer[3:]
        weights = [
            w * jnp.where(chip_of[n] < chip_of[m], clear, 1.0) for m, w in enumerate(weights)
        ]
        own = jnp.ones_like(clear)
        for m in range(n):
            own = own * jnp.where(chip_of[m] < chip_of[n], 1.0 - got[m][3:], 1.0)
        weights.append(own)
    return sum(w * layer for w, layer in zip(weights, got))


def vmem(count):
    return [pl.BlockSpec(memory_space=pltpu.VMEM)] * count


def held(*dims):
    return pltpu.VMEM(dims, F32)


def in_vmem(x):
    return pltpu.with_memory_space_constraint(x, pltpu.VMEM)


def per_device(velocity, metric, colour_map, counts):
    _, slab, ny, cx = velocity.shape
    devices = lax.axis_size("depth")
    tiles = lax.axis_size("tile")
    total_depth = slab * devices
    scalars = pl.BlockSpec(memory_space=pltpu.SMEM)

    def limit(size):
        return pltpu.CompilerParams(vmem_limit_bytes=size * MIB)

    hbm = pl.BlockSpec(memory_space=pltpu.HBM)
    share = ny // devices
    spare = SUB if share < SUB else 0
    padded = (3, slab + 2 * REACH, ny + 2 * SUB, cx)
    columns = (3, ny // 2, cx)
    up = [(i, (i + 1) % devices) for i in range(devices)]
    down = [(i, (i - 1) % devices) for i in range(devices)]
    whole = pltpu.with_memory_space_constraint(velocity, pltpu.HBM)
    near, far = pl.pallas_call(
        ends_kernel,
        out_shape=(held(3, REACH, ny, cx), held(3, REACH, ny + spare, cx)),
        in_specs=[hbm],
        out_specs=tuple(vmem(2)),
        scratch_shapes=[pltpu.SemaphoreType.DMA((2,))],
        compiler_params=limit(4),
        name="ends",
    )(whole)
    near = lax.ppermute(near, "depth", [(down if i % 2 else up)[i] for i in range(devices)])
    far = lax.ppermute(far, "depth", [(up if i % 2 else down)[i] for i in range(devices)])

    ext, to_right, to_left = pl.pallas_call(
        edges_kernel,
        out_shape=(held(*padded), held(*columns), held(*columns)),
        in_specs=vmem(1),
        out_specs=tuple(vmem(3)),
        scratch_shapes=[pltpu.SemaphoreType.DMA((1,))],
        compiler_params=limit(4),
        name="edges",
    )(velocity)
    from_left = lax.ppermute(to_right, "tile", [(i, (i + 1) % tiles) for i in range(tiles)])
    from_right = lax.ppermute(to_left, "tile", [(i, (i - 1) % tiles) for i in range(tiles)])

    stream, span, outline = pl.pallas_call(
        slopes_kernel,
        out_shape=(
            held(3, slab, ny, cx),
            held(4, slab, ny, cx),
            held(6, REACH, ny + spare, cx),
        ),
        in_specs=vmem(2) + [scalars],
        out_specs=tuple(vmem(3)),
        scratch_shapes=[pltpu.VMEM((2 * cx, cx), BF16)],
        compiler_params=limit(4),
        name="slopes",
    )(in_vmem(ext), in_vmem(near), metric)

    part, stream = pl.pallas_call(
        functools.partial(inner_kernel, total_depth),
        out_shape=(held(4, ny + spare, cx), held(3, REACH, ny + spare, cx)),
        in_specs=vmem(6),
        out_specs=tuple(vmem(2)),
        scratch_shapes=[
            pltpu.VMEM((3 * ny, slab * cx), F32),
            pltpu.VMEM((3 * ny, 2 * cx), BF16),
            pltpu.VMEM((2 * cx, cx), F32),
        ],
        compiler_params=limit(8),
        name="inner",
    )(*map(in_vmem, (stream, span, from_left, from_right, counts, colour_map)))

    tall = jnp.pad(counts, ((0, spare), (0, 0))) if spare else counts
    rest = tuple(map(in_vmem, (far, outline, stream, part, tall, colour_map)))

    def outer(own, name):
        return pl.pallas_call(
            functools.partial(outer_kernel, total_depth, own),
            out_shape=held(devices // 2, 4, share, cx),
            in_specs=vmem(6),
            out_specs=vmem(1)[0],
            compiler_params=limit(4),
            name=name,
        )(*rest)

    theirs = outer(False, "theirs")
    return gather_rays(outer(True, "mine"), theirs)


def solution(mesh):
    in_specs = (P(None, "depth", None, "tile"), P(), P(), P(None, "tile"))
    out_specs = P(None, "depth", "tile")
    return jax.shard_map(
        per_device, mesh=mesh, in_specs=in_specs, out_specs=out_specs, check_vma=False
    )
```

```python
import functools
import math

import jax
import jax.numpy as jnp
from jax import lax
from jax.experimental import pallas as pl
from jax.experimental.pallas import tpu as pltpu
from jax.sharding import PartitionSpec as P

REACH = 3
SUB = 8
GROUP = 8
CRITERION_SCALE = 2.0
VORTEX_SCALE = 4.0
OPTICAL_DEPTH = 4.0
LOG2_E = 1.4426950408889634
TINY = 1.2e-38
FIELD = 13
UNIT = 4096.0
MIB = 1024 * 1024
F32 = jnp.float32
BF16 = jnp.bfloat16


def parity():
    return lax.rem(lax.axis_index("depth"), 2)


def stencil(ahead, behind):
    return 45.0 * (ahead[0] - behind[0]) - 9.0 * (ahead[1] - behind[1]) + (ahead[2] - behind[2])


def weight_of(distance):
    out = jnp.zeros(distance.shape, F32)
    for k, weight in ((1, 45.0), (2, -9.0), (3, 1.0)):
        out = jnp.where(distance == k, weight, out)
        out = jnp.where(distance == -k, -weight, out)
    return out


def halves(x):
    high = x.astype(BF16)
    low = (x - high.astype(F32)).astype(BF16)
    return jnp.concatenate([high, low], axis=1)


def ends_kernel(vel, near, far, sems):
    odd = parity()
    last = vel.shape[1] - REACH
    rows = pl.ds(0, vel.shape[2])
    copies = [
        pltpu.make_async_copy(
            vel.at[:, pl.ds(odd * last, REACH)], far.at[:, :, rows, :], sems.at[0]),
        pltpu.make_async_copy(vel.at[:, pl.ds((1 - odd) * last, REACH)], near, sems.at[1]),
    ]
    for copy in copies:
        copy.start()
    for copy in copies:
        copy.wait()


def edges_kernel(vel, ext, right_out, left_out, sem):
    slab, ny, cx = vel.shape[1:]
    half = ny // 2
    body = pl.ds(SUB, ny)
    copy = pltpu.make_async_copy(vel, ext.at[:, pl.ds(REACH, slab), body, :], sem.at[0])
    copy.start()
    zero = jnp.zeros((SUB, cx), F32)
    steps = half // SUB
    layers = -(-slab // steps)
    lane = lax.broadcasted_iota(jnp.int32, (SUB, cx), 1)

    def tile(t, _):
        for c in range(3):
            for k in range(layers):
                z = REACH + jnp.minimum(t * layers + k, slab - 1)
                ext[c, z, pl.ds(0, SUB), :] = zero
                ext[c, z, pl.ds(ny + SUB, SUB), :] = zero
            for z in range(REACH):
                for h in range(2):
                    rows = pl.ds(pl.multiple_of(SUB + h * half + t * SUB, SUB), SUB)
                    ext[c, z, rows, :] = zero
                    ext[c, REACH + slab + z, rows, :] = zero
            to_right = jnp.zeros((SUB, cx), F32)
            to_left = jnp.zeros((SUB, cx), F32)
            for z in range(slab):
                for h in range(2):
                    first = GROUP * z + 4 * h
                    rows = pl.ds(pl.multiple_of(h * half + t * SUB, SUB), SUB)
                    turned = pltpu.roll(vel[c, z, rows, :], (first + REACH) % cx, 1)
                    to_right = jnp.where((lane >= first) & (lane < first + 4), turned, to_right)
                    place = lax.rem(lane + (2 * cx - first - REACH), cx)
                    to_left = jnp.where(place < 4, turned, to_left)
            rows = pl.ds(pl.multiple_of(t * SUB, SUB), SUB)
            right_out[c, rows, :] = to_right
            left_out[c, rows, :] = to_left
        return 0

    lax.fori_loop(0, half // SUB, tile, 0)
    copy.wait()


def slopes_kernel(ext, near, metric, stream, span, outline, band):
    slab, ny, cx = stream.shape[1:]
    odd = parity()
    body = pl.ds(SUB, ny)
    source = lax.broadcasted_iota(jnp.int32, (cx, cx), 0)
    target = lax.broadcasted_iota(jnp.int32, (cx, cx), 1)
    weights = weight_of(source - target).astype(BF16)
    band[pl.ds(0, cx), :] = weights
    band[pl.ds(cx, cx), :] = weights
    row = lax.broadcasted_iota(jnp.int32, (SUB, cx), 0)
    sign = jnp.full((SUB, cx), 1 - 2 * odd, jnp.int32).astype(F32)
    reach = [45.0 * sign, -9.0 * sign, sign]
    steps = math.gcd(slab, ny // SUB, 1)
    layers = slab // steps
    tiles = ny // SUB // steps

    def along(z):
        rows = jnp.concatenate([halves(ext[c, REACH + z, body, :]) for c in range(3)], axis=0)
        out = jnp.dot(rows, band[...], preferred_element_type=F32)
        for c in range(3):
            stream[c, z] = out[c * ny : (c + 1) * ny]

    def tile(t):
        base = pl.multiple_of(t * SUB, SUB)
        rows = pl.ds(base, SUB)
        inner = pl.ds(base + SUB, SUB)
        scale = jnp.zeros((SUB, cx), F32)
        for r in range(SUB):
            scale = jnp.where(row == r, metric[base + r], scale)

        def slopes(z):
            dy = [
                scale * stencil(
                    [ext[c, REACH + z, pl.ds(base + SUB + k, SUB), :] for k in (1, 2, 3)],
                    [ext[c, REACH + z, pl.ds(base + SUB - k, SUB), :] for k in (1, 2, 3)],
                )
                for c in range(3)
            ]
            dz = [
                stencil(
                    [ext[c, REACH + z + k, inner, :] for k in (1, 2, 3)],
                    [ext[c, REACH + z - k, inner, :] for k in (1, 2, 3)],
                )
                for c in range(3)
            ]
            return dy, dz

        def keep(z, dy, dz):
            turn = dy[2] - dz[1]
            span[0, z, rows, :] = dy[0]
            span[1, z, rows, :] = dz[0]
            span[2, z, rows, :] = dy[1] * dy[1] + dz[2] * dz[2] + 2.0 * (dy[2] * dz[1])
            span[3, z, rows, :] = turn * turn

        for z in range(REACH, slab - REACH):
            keep(z, *slopes(z))
        beyond = [[near[c, odd * (2 - 2 * r) + r, rows, :] for r in range(REACH)] for c in range(3)]
        for q in range(REACH):
            low, high = q, slab - 1 - q
            z = odd * (low - high) + high
            dy, dz = slopes(z)
            for c in range(3):
                for r in range(REACH - q):
                    dz[c] = dz[c] + reach[q + r] * beyond[c][r]
            keep(z, dy, dz)
            dy, dz = slopes(odd * (high - low) + low)
            for c in range(3):
                outline[c, q, rows, :] = dy[c]
                outline[3 + c, q, rows, :] = dz[c]

    def step(s, _):
        for k in range(layers):
            along(s * layers + k)
        for k in range(tiles):
            tile(s * tiles + k)
        return 0

    lax.fori_loop(0, steps, step, 0)


def tables(colour_map):
    bins = colour_map.shape[1]
    table = colour_map[...].astype(F32) * UNIT
    after = pltpu.roll(table, bins - 1, 1)
    packed = table.astype(jnp.int32) * (1 << FIELD) + after.astype(jnp.int32)
    return [jnp.broadcast_to(packed[k : k + 1], (SUB, bins)) for k in range(4)]


def shade(square, spin, seen, pairs, total_depth):
    bins = pairs[0].shape[1]
    half_top = (bins - 1) * 0.5
    level = half_top + half_top * jnp.tanh(square * (-0.5 / (3600.0 * CRITERION_SCALE)))
    low = jnp.minimum(jnp.floor(level), bins - 2.0)
    fraction = level - low
    index = low.astype(jnp.int32)

    def value(k):
        pair = jnp.take_along_axis(pairs[k], index, axis=1, mode="promise_in_bounds")
        first = lax.shift_right_logical(pair, FIELD).astype(F32)
        second = (pair & ((1 << FIELD) - 1)).astype(F32)
        return first + fraction * (second - first)

    gain = -LOG2_E * OPTICAL_DEPTH / (total_depth * UNIT)
    passed = jnp.exp2(jnp.where(seen, value(0) * gain, 0.0))
    length = spin * lax.rsqrt(jnp.maximum(spin, TINY))
    strength = jnp.tanh(length * (1.0 / (60.0 * VORTEX_SCALE)))
    return passed, [value(k) for k in (1, 2, 3)], strength


def inner_kernel(
    total_depth, stream, span, from_left, from_right, counts, colour_map,
    part, stream_out, terms, packed, place,
):
    slab, ny, cx = stream.shape[1:]
    half = ny // 2
    odd = parity()
    lane = lax.broadcasted_iota(jnp.int32, (SUB, cx), 1)
    within = lax.rem(lane, GROUP)

    def pack(t, _):
        rows = pl.ds(pl.multiple_of(2 * t * SUB, 2 * SUB), 2 * SUB)
        wide = lax.rem(lax.broadcasted_iota(jnp.int32, (2 * SUB, cx), 1), GROUP)
        for c in range(3):
            right = from_left[c, rows, :]
            left = from_right[c, rows, :]
            first = jnp.where(wide < 3, right, left)
            second = pltpu.roll(jnp.where((wide >= 4) & (wide < 7), right, left), cx - 4, 1)
            at = pl.multiple_of(c * ny + 2 * t * SUB, 2 * SUB)
            packed[pl.ds(at, 2 * SUB), :] = halves(first)
            packed[pl.ds(pl.multiple_of(at + half, 2 * SUB), 2 * SUB), :] = halves(second)
        return 0

    lax.fori_loop(0, half // (2 * SUB), pack, 0)
    place[...] = jnp.zeros(place.shape, F32)
    source = lax.broadcasted_iota(jnp.int32, (SUB, cx), 0)
    column = jnp.where(source < REACH, source - REACH, source - REACH + cx)
    weights = weight_of(column - lane)
    place[pl.ds(cx, SUB), :] = jnp.where(source < 2 * REACH, weights, 0.0)

    start = REACH * (1 - odd)
    together = math.gcd(slab, 16)

    def layers(s, _):
        spread = jnp.concatenate(
            [
                place[
                    pl.ds(
                        pl.multiple_of(
                            cx - GROUP * lax.rem(start + s * together + k, slab), SUB), cx), :
                ].astype(BF16)
                for k in range(together)
            ],
            axis=1,
        )
        columns = pl.ds(pl.multiple_of(s * together * cx, together * cx), together * cx)
        terms[:, columns] = jnp.dot(
            packed[...], jnp.concatenate([spread, spread], axis=0), preferred_element_type=F32
        )
        return 0

    lax.fori_loop(0, slab // together, layers, 0)

    def along(c, z, cell, rows, at):
        return stream[c, z, rows, :] + terms[at, cell * cx : (cell + 1) * cx]

    for k in range(REACH):
        cell = slab - REACH + k
        for c in range(3):
            stream_out[c, odd * (2 - 2 * k) + k, pl.ds(0, ny), :] = along(
                c, lax.rem(start + cell, slab), cell, slice(None), pl.ds(c * ny, ny))

    pairs = tables(colour_map)
    first_depth = lax.axis_index("depth") * slab + start

    def tile(t):
        rows = pl.ds(pl.multiple_of(t * SUB, SUB), SUB)
        count = counts[rows, :] - first_depth
        colour = [jnp.zeros((SUB, cx), F32) for _ in range(3)]
        clear = jnp.ones((SUB, cx), F32)
        for cell in range(slab - REACH):
            dx = [
                along(c, start + cell, cell, rows, pl.ds(pl.multiple_of(c * ny + t * SUB, SUB), SUB))
                for c in range(3)
            ]
            dy, dz, rest, turn = [span[k, start + cell, rows, :] for k in range(4)]
            square = rest + dx[0] * dx[0] + 2.0 * (dy * dx[1] + dz * dx[2])
            w1 = dz - dx[2]
            w2 = dx[1] - dy
            spin = turn + w1 * w1 + w2 * w2
            passed, values, strength = shade(square, spin, count > cell, pairs, total_depth)
            after = clear * passed
            weight = (clear - after) * strength
            colour = [colour[k] + weight * values[k] for k in range(3)]
            clear = after
        for k in range(3):
            part[k, rows, :] = colour[k] * (1.0 / UNIT)
        part[3, rows, :] = clear

    unroll = math.gcd(ny // SUB, 12)

    def tiles(s, _):
        for k in range(unroll):
            tile(s * unroll + k)
        return 0

    lax.fori_loop(0, ny // SUB // unroll, tiles, 0)


def owner_chip(chip, k, chips):
    return chip ^ k if chips in (2, 4) else lax.rem(chip + k, chips)


def outer_kernel(total_depth, own, far, outline, stream, part, counts, colour_map, out):
    chips, _, share, cx = out.shape
    odd = parity()
    me = lax.axis_index("depth")
    slab = total_depth // lax.axis_size("depth")
    pairs = tables(colour_map)
    sign = jnp.full((SUB, cx), 2 * odd - 1, jnp.int32).astype(F32)
    front = jnp.full((SUB, cx), odd, jnp.int32) == 0
    weights = [45.0 * sign, -9.0 * sign, sign]

    def window(rows):
        count = counts[rows, :] - me * slab
        beyond = [
            [far[c, (1 - odd) * (2 - 2 * r) + r, rows, :] for r in range(REACH)]
            for c in range(3)
        ]
        layers = []
        for q in range(REACH):
            dx = [stream[c, q, rows, :] for c in range(3)]
            dy = [outline[c, q, rows, :] for c in range(3)]
            dz = [outline[3 + c, q, rows, :] for c in range(3)]
            for c in range(3):
                for r in range(REACH - q):
                    dz[c] = dz[c] + weights[q + r] * beyond[c][r]
            w0 = dy[2] - dz[1]
            w1 = dz[0] - dx[2]
            w2 = dx[1] - dy[0]
            square = dx[0] * dx[0] + dy[1] * dy[1] + dz[2] * dz[2]
            square = square + 2.0 * (dy[0] * dx[1] + dz[0] * dx[2] + dz[1] * dy[2])
            spin = w0 * w0 + w1 * w1 + w2 * w2
            seen = count > odd * (slab - 1 - 2 * q) + q
            passed, values, strength = shade(square, spin, seen, pairs, total_depth)
            weight = (1.0 - passed) * (strength * (1.0 / UNIT))
            layers.append([weight * value for value in values] + [passed])
        first = [jnp.where(front, a, b) for a, b in zip(layers[0], layers[2])]
        last = [jnp.where(front, b, a) for a, b in zip(layers[0], layers[2])]
        clear = first[3] * layers[1][3]
        rest = part[3, rows, :]
        outer_clear = clear * last[3]
        image = []
        for k in range(3):
            edge = first[k] + first[3] * layers[1][k] + clear * last[k]
            inner = part[k, rows, :]
            image.append(jnp.where(front, edge + outer_clear * inner, inner + rest * edge))
        return image + [1.0 - outer_clear * rest]

    owner = odd if own else 1 - odd
    starts = sorted({min(w, max(share - SUB, 0)) for w in range(0, share, SUB)})
    height = min(share, SUB)
    for s in range(chips):
        chip = owner_chip(me // 2, s, chips)
        for w in starts:
            row = (2 * chip + owner) * share + w
            image = window(pl.ds(row, SUB))
            for k in range(4):
                out[s, k, pl.ds(w, height), :] = image[k][:height]


def over(front, back):
    return front + (1.0 - front[..., 3:, :, :]) * back


def gather_rays(mine, theirs):
    chips = mine.shape[0]
    devices = 2 * chips
    me = lax.axis_index("depth")
    odd = lax.rem(me, 2) == 1
    theirs = lax.ppermute(theirs, "depth", [(i, i + 1 - 2 * (i % 2)) for i in range(devices)])
    both = over(jnp.where(odd, theirs, mine), jnp.where(odd, mine, theirs))
    chip = me // 2
    if chips in (2, 4):
        step, source = (2, 1, 3), lambda k: chip ^ k
        rings = {k: [(i, i ^ (2 * k)) for i in range(devices)] for k in range(1, chips)}
    else:
        step, source = range(1, chips), lambda k: lax.rem(chip - k + chips, chips)
        rings = {k: [(i, (i + 2 * k) % devices) for i in range(devices)] for k in range(1, chips)}
    order = [0] + [k for k in step if k < chips]
    got = [both[0]] + [lax.ppermute(both[k], "depth", rings[k]) for k in order[1:]]
    chip_of = [source(k) for k in order]
    weights, image = [], 0.0
    for n, layer in enumerate(got):
        clear = 1.0 - layer[3:]
        weights = [
            w * jnp.where(chip_of[n] < chip_of[m], clear, 1.0) for m, w in enumerate(weights)
        ]
        own = jnp.ones_like(clear)
        for m in range(n):
            own = own * jnp.where(chip_of[m] < chip_of[n], 1.0 - got[m][3:], 1.0)
        weights.append(own)
    return sum(w * layer for w, layer in zip(weights, got))


def vmem(count):
    return [pl.BlockSpec(memory_space=pltpu.VMEM)] * count


def held(*dims):
    return pltpu.VMEM(dims, F32)


def in_vmem(x):
    return pltpu.with_memory_space_constraint(x, pltpu.VMEM)


def per_device(velocity, metric, colour_map, counts):
    _, slab, ny, cx = velocity.shape
    devices = lax.axis_size("depth")
    tiles = lax.axis_size("tile")
    total_depth = slab * devices
    scalars = pl.BlockSpec(memory_space=pltpu.SMEM)

    def limit(size):
        return pltpu.CompilerParams(vmem_limit_bytes=size * MIB)

    hbm = pl.BlockSpec(memory_space=pltpu.HBM)
    share = ny // devices
    spare = SUB if share < SUB else 0
    padded = (3, slab + 2 * REACH, ny + 2 * SUB, cx)
    columns = (3, ny // 2, cx)
    up = [(i, (i + 1) % devices) for i in range(devices)]
    down = [(i, (i - 1) % devices) for i in range(devices)]
    whole = pltpu.with_memory_space_constraint(velocity, pltpu.HBM)
    near, far = pl.pallas_call(
        ends_kernel,
        out_shape=(held(3, REACH, ny, cx), held(3, REACH, ny + spare, cx)),
        in_specs=[hbm],
        out_specs=tuple(vmem(2)),
        scratch_shapes=[pltpu.SemaphoreType.DMA((2,))],
        compiler_params=limit(4),
        name="ends",
    )(whole)
    near = lax.ppermute(near, "depth", [(down if i % 2 else up)[i] for i in range(devices)])
    far = lax.ppermute(far, "depth", [(up if i % 2 else down)[i] for i in range(devices)])

    ext, to_right, to_left = pl.pallas_call(
        edges_kernel,
        out_shape=(held(*padded), held(*columns), held(*columns)),
        in_specs=vmem(1),
        out_specs=tuple(vmem(3)),
        scratch_shapes=[pltpu.SemaphoreType.DMA((1,))],
        compiler_params=limit(4),
        name="edges",
    )(velocity)
    from_left = lax.ppermute(to_right, "tile", [(i, (i + 1) % tiles) for i in range(tiles)])
    from_right = lax.ppermute(to_left, "tile", [(i, (i - 1) % tiles) for i in range(tiles)])

    stream, span, outline = pl.pallas_call(
        slopes_kernel,
        out_shape=(
            held(3, slab, ny, cx),
            held(4, slab, ny, cx),
            held(6, REACH, ny + spare, cx),
        ),
        in_specs=vmem(2) + [scalars],
        out_specs=tuple(vmem(3)),
        scratch_shapes=[pltpu.VMEM((2 * cx, cx), BF16)],
        compiler_params=limit(4),
        name="slopes",
    )(in_vmem(ext), in_vmem(near), metric)

    part, stream = pl.pallas_call(
        functools.partial(inner_kernel, total_depth),
        out_shape=(held(4, ny + spare, cx), held(3, REACH, ny + spare, cx)),
        in_specs=vmem(6),
        out_specs=tuple(vmem(2)),
        scratch_shapes=[
            pltpu.VMEM((3 * ny, slab * cx), F32),
            pltpu.VMEM((3 * ny, 2 * cx), BF16),
            pltpu.VMEM((2 * cx, cx), F32),
        ],
        compiler_params=limit(8),
        name="inner",
    )(*map(in_vmem, (stream, span, from_left, from_right, counts, colour_map)))

    tall = jnp.pad(counts, ((0, spare), (0, 0))) if spare else counts
    rest = tuple(map(in_vmem, (far, outline, stream, part, tall, colour_map)))

    def outer(own, name):
        return pl.pallas_call(
            functools.partial(outer_kernel, total_depth, own),
            out_shape=held(devices // 2, 4, share, cx),
            in_specs=vmem(6),
            out_specs=vmem(1)[0],
            compiler_params=limit(4),
            name=name,
        )(*rest)

    theirs = outer(False, "theirs")
    return gather_rays(outer(True, "mine"), theirs)


def solution(mesh):
    in_specs = (P(None, "depth", None, "tile"), P(), P(), P(None, "tile"))
    out_specs = P(None, "depth", "tile")
    return jax.shard_map(
        per_device, mesh=mesh, in_specs=in_specs, out_specs=out_specs, check_vma=False
    )
```

```python
import functools
import math

import jax
import jax.numpy as jnp
from jax import lax
from jax.experimental import pallas as pl
from jax.experimental.pallas import tpu as pltpu
from jax.sharding import PartitionSpec as P

REACH = 3
SUB = 8
GROUP = 8
CRITERION_SCALE = 2.0
VORTEX_SCALE = 4.0
OPTICAL_DEPTH = 4.0
LOG2_E = 1.4426950408889634
TINY = 1.2e-38
FIELD = 13
UNIT = 4096.0
MIB = 1024 * 1024
F32 = jnp.float32
BF16 = jnp.bfloat16


def parity():
    return lax.rem(lax.axis_index("depth"), 2)


def stencil(ahead, behind):
    return 45.0 * (ahead[0] - behind[0]) - 9.0 * (ahead[1] - behind[1]) + (ahead[2] - behind[2])


def weight_of(distance):
    out = jnp.zeros(distance.shape, F32)
    for k, weight in ((1, 45.0), (2, -9.0), (3, 1.0)):
        out = jnp.where(distance == k, weight, out)
        out = jnp.where(distance == -k, -weight, out)
    return out


def halves(x):
    high = x.astype(BF16)
    low = (x - high.astype(F32)).astype(BF16)
    return jnp.concatenate([high, low], axis=1)


def ends_kernel(vel, near, far, sems):
    odd = parity()
    last = vel.shape[1] - REACH
    rows = pl.ds(0, vel.shape[2])
    copies = [
        pltpu.make_async_copy(
            vel.at[:, pl.ds(odd * last, REACH)], far.at[:, :, rows, :], sems.at[0]),
        pltpu.make_async_copy(vel.at[:, pl.ds((1 - odd) * last, REACH)], near, sems.at[1]),
    ]
    for copy in copies:
        copy.start()
    for copy in copies:
        copy.wait()


def edges_kernel(vel, ext, right_out, left_out, sem):
    slab, ny, cx = vel.shape[1:]
    half = ny // 2
    body = pl.ds(SUB, ny)
    copy = pltpu.make_async_copy(vel, ext.at[:, pl.ds(REACH, slab), body, :], sem.at[0])
    copy.start()
    zero = jnp.zeros((SUB, cx), F32)
    steps = half // SUB
    layers = -(-slab // steps)
    lane = lax.broadcasted_iota(jnp.int32, (SUB, cx), 1)

    def tile(t, _):
        for c in range(3):
            for k in range(layers):
                z = REACH + jnp.minimum(t * layers + k, slab - 1)
                ext[c, z, pl.ds(0, SUB), :] = zero
                ext[c, z, pl.ds(ny + SUB, SUB), :] = zero
            for z in range(REACH):
                for h in range(2):
                    rows = pl.ds(pl.multiple_of(SUB + h * half + t * SUB, SUB), SUB)
                    ext[c, z, rows, :] = zero
                    ext[c, REACH + slab + z, rows, :] = zero
            to_right = jnp.zeros((SUB, cx), F32)
            to_left = jnp.zeros((SUB, cx), F32)
            for z in range(slab):
                for h in range(2):
                    first = GROUP * z + 4 * h
                    rows = pl.ds(pl.multiple_of(h * half + t * SUB, SUB), SUB)
                    turned = pltpu.roll(vel[c, z, rows, :], (first + REACH) % cx, 1)
                    to_right = jnp.where((lane >= first) & (lane < first + 4), turned, to_right)
                    place = lax.rem(lane + (2 * cx - first - REACH), cx)
                    to_left = jnp.where(place < 4, turned, to_left)
            rows = pl.ds(pl.multiple_of(t * SUB, SUB), SUB)
            right_out[c, rows, :] = to_right
            left_out[c, rows, :] = to_left
        return 0

    lax.fori_loop(0, half // SUB, tile, 0, unroll=True)
    copy.wait()


def slopes_kernel(ext, near, metric, stream, span, outline, band):
    slab, ny, cx = stream.shape[1:]
    odd = parity()
    body = pl.ds(SUB, ny)
    source = lax.broadcasted_iota(jnp.int32, (cx, cx), 0)
    target = lax.broadcasted_iota(jnp.int32, (cx, cx), 1)
    weights = weight_of(source - target).astype(BF16)
    band[pl.ds(0, cx), :] = weights
    band[pl.ds(cx, cx), :] = weights
    row = lax.broadcasted_iota(jnp.int32, (SUB, cx), 0)
    sign = jnp.full((SUB, cx), 1 - 2 * odd, jnp.int32).astype(F32)
    reach = [45.0 * sign, -9.0 * sign, sign]
    steps = math.gcd(slab, ny // SUB, 1)
    layers = slab // steps
    tiles = ny // SUB // steps

    def along(z):
        rows = jnp.concatenate([halves(ext[c, REACH + z, body, :]) for c in range(3)], axis=0)
        out = jnp.dot(rows, band[...], preferred_element_type=F32)
        for c in range(3):
            stream[c, z] = out[c * ny : (c + 1) * ny]

    def tile(t):
        base = pl.multiple_of(t * SUB, SUB)
        rows = pl.ds(base, SUB)
        inner = pl.ds(base + SUB, SUB)
        scale = jnp.zeros((SUB, cx), F32)
        for r in range(SUB):
            scale = jnp.where(row == r, metric[base + r], scale)

        def slopes(z):
            dy = [
                scale * stencil(
                    [ext[c, REACH + z, pl.ds(base + SUB + k, SUB), :] for k in (1, 2, 3)],
                    [ext[c, REACH + z, pl.ds(base + SUB - k, SUB), :] for k in (1, 2, 3)],
                )
                for c in range(3)
            ]
            dz = [
                stencil(
                    [ext[c, REACH + z + k, inner, :] for k in (1, 2, 3)],
                    [ext[c, REACH + z - k, inner, :] for k in (1, 2, 3)],
                )
                for c in range(3)
            ]
            return dy, dz

        def keep(z, dy, dz):
            turn = dy[2] - dz[1]
            span[0, z, rows, :] = dy[0]
            span[1, z, rows, :] = dz[0]
            span[2, z, rows, :] = dy[1] * dy[1] + dz[2] * dz[2] + 2.0 * (dy[2] * dz[1])
            span[3, z, rows, :] = turn * turn

        for z in range(REACH, slab - REACH):
            keep(z, *slopes(z))
        beyond = [[near[c, odd * (2 - 2 * r) + r, rows, :] for r in range(REACH)] for c in range(3)]
        for q in range(REACH):
            low, high = q, slab - 1 - q
            z = odd * (low - high) + high
            dy, dz = slopes(z)
            for c in range(3):
                for r in range(REACH - q):
                    dz[c] = dz[c] + reach[q + r] * beyond[c][r]
            keep(z, dy, dz)
            dy, dz = slopes(odd * (high - low) + low)
            for c in range(3):
                outline[c, q, rows, :] = dy[c]
                outline[3 + c, q, rows, :] = dz[c]

    def step(s, _):
        for k in range(layers):
            along(s * layers + k)
        for k in range(tiles):
            tile(s * tiles + k)
        return 0

    lax.fori_loop(0, steps, step, 0)


def tables(colour_map):
    bins = colour_map.shape[1]
    table = colour_map[...].astype(F32) * UNIT
    after = pltpu.roll(table, bins - 1, 1)
    packed = table.astype(jnp.int32) * (1 << FIELD) + after.astype(jnp.int32)
    return [jnp.broadcast_to(packed[k : k + 1], (SUB, bins)) for k in range(4)]


def shade(square, spin, seen, pairs, total_depth):
    bins = pairs[0].shape[1]
    half_top = (bins - 1) * 0.5
    level = half_top + half_top * jnp.tanh(square * (-0.5 / (3600.0 * CRITERION_SCALE)))
    low = jnp.minimum(jnp.floor(level), bins - 2.0)
    fraction = level - low
    index = low.astype(jnp.int32)

    def value(k):
        pair = jnp.take_along_axis(pairs[k], index, axis=1, mode="promise_in_bounds")
        first = lax.shift_right_logical(pair, FIELD).astype(F32)
        second = (pair & ((1 << FIELD) - 1)).astype(F32)
        return first + fraction * (second - first)

    gain = -LOG2_E * OPTICAL_DEPTH / (total_depth * UNIT)
    passed = jnp.exp2(jnp.where(seen, value(0) * gain, 0.0))
    length = spin * lax.rsqrt(jnp.maximum(spin, TINY))
    strength = jnp.tanh(length * (1.0 / (60.0 * VORTEX_SCALE)))
    return passed, [value(k) for k in (1, 2, 3)], strength


def inner_kernel(
    total_depth, stream, span, from_left, from_right, counts, colour_map,
    part, stream_out, terms, packed, place,
):
    slab, ny, cx = stream.shape[1:]
    half = ny // 2
    odd = parity()
    lane = lax.broadcasted_iota(jnp.int32, (SUB, cx), 1)
    within = lax.rem(lane, GROUP)

    def pack(t, _):
        rows = pl.ds(pl.multiple_of(2 * t * SUB, 2 * SUB), 2 * SUB)
        wide = lax.rem(lax.broadcasted_iota(jnp.int32, (2 * SUB, cx), 1), GROUP)
        for c in range(3):
            right = from_left[c, rows, :]
            left = from_right[c, rows, :]
            first = jnp.where(wide < 3, right, left)
            second = pltpu.roll(jnp.where((wide >= 4) & (wide < 7), right, left), cx - 4, 1)
            at = pl.multiple_of(c * ny + 2 * t * SUB, 2 * SUB)
            packed[pl.ds(at, 2 * SUB), :] = halves(first)
            packed[pl.ds(pl.multiple_of(at + half, 2 * SUB), 2 * SUB), :] = halves(second)
        return 0

    lax.fori_loop(0, half // (2 * SUB), pack, 0)
    place[...] = jnp.zeros(place.shape, F32)
    source = lax.broadcasted_iota(jnp.int32, (SUB, cx), 0)
    column = jnp.where(source < REACH, source - REACH, source - REACH + cx)
    weights = weight_of(column - lane)
    place[pl.ds(cx, SUB), :] = jnp.where(source < 2 * REACH, weights, 0.0)

    start = REACH * (1 - odd)
    together = math.gcd(slab, 16)

    def layers(s, _):
        spread = jnp.concatenate(
            [
                place[
                    pl.ds(
                        pl.multiple_of(
                            cx - GROUP * lax.rem(start + s * together + k, slab), SUB), cx), :
                ].astype(BF16)
                for k in range(together)
            ],
            axis=1,
        )
        columns = pl.ds(pl.multiple_of(s * together * cx, together * cx), together * cx)
        terms[:, columns] = jnp.dot(
            packed[...], jnp.concatenate([spread, spread], axis=0), preferred_element_type=F32
        )
        return 0

    lax.fori_loop(0, slab // together, layers, 0)

    def along(c, z, cell, rows, at):
        return stream[c, z, rows, :] + terms[at, cell * cx : (cell + 1) * cx]

    for k in range(REACH):
        cell = slab - REACH + k
        for c in range(3):
            stream_out[c, odd * (2 - 2 * k) + k, pl.ds(0, ny), :] = along(
                c, lax.rem(start + cell, slab), cell, slice(None), pl.ds(c * ny, ny))

    pairs = tables(colour_map)
    first_depth = lax.axis_index("depth") * slab + start

    def tile(t):
        rows = pl.ds(pl.multiple_of(t * SUB, SUB), SUB)
        count = counts[rows, :] - first_depth
        colour = [jnp.zeros((SUB, cx), F32) for _ in range(3)]
        clear = jnp.ones((SUB, cx), F32)
        for cell in range(slab - REACH):
            dx = [
                along(c, start + cell, cell, rows, pl.ds(pl.multiple_of(c * ny + t * SUB, SUB), SUB))
                for c in range(3)
            ]
            dy, dz, rest, turn = [span[k, start + cell, rows, :] for k in range(4)]
            square = rest + dx[0] * dx[0] + 2.0 * (dy * dx[1] + dz * dx[2])
            w1 = dz - dx[2]
            w2 = dx[1] - dy
            spin = turn + w1 * w1 + w2 * w2
            passed, values, strength = shade(square, spin, count > cell, pairs, total_depth)
            after = clear * passed
            weight = (clear - after) * strength
            colour = [colour[k] + weight * values[k] for k in range(3)]
            clear = after
        for k in range(3):
            part[k, rows, :] = colour[k] * (1.0 / UNIT)
        part[3, rows, :] = clear

    unroll = math.gcd(ny // SUB, 12)

    def tiles(s, _):
        for k in range(unroll):
            tile(s * unroll + k)
        return 0

    lax.fori_loop(0, ny // SUB // unroll, tiles, 0)


def owner_chip(chip, k, chips):
    return chip ^ k if chips in (2, 4) else lax.rem(chip + k, chips)


def outer_kernel(total_depth, own, far, outline, stream, part, counts, colour_map, out):
    chips, _, share, cx = out.shape
    odd = parity()
    me = lax.axis_index("depth")
    slab = total_depth // lax.axis_size("depth")
    pairs = tables(colour_map)
    sign = jnp.full((SUB, cx), 2 * odd - 1, jnp.int32).astype(F32)
    front = jnp.full((SUB, cx), odd, jnp.int32) == 0
    weights = [45.0 * sign, -9.0 * sign, sign]

    def window(rows):
        count = counts[rows, :] - me * slab
        beyond = [
            [far[c, (1 - odd) * (2 - 2 * r) + r, rows, :] for r in range(REACH)]
            for c in range(3)
        ]
        layers = []
        for q in range(REACH):
            dx = [stream[c, q, rows, :] for c in range(3)]
            dy = [outline[c, q, rows, :] for c in range(3)]
            dz = [outline[3 + c, q, rows, :] for c in range(3)]
            for c in range(3):
                for r in range(REACH - q):
                    dz[c] = dz[c] + weights[q + r] * beyond[c][r]
            w0 = dy[2] - dz[1]
            w1 = dz[0] - dx[2]
            w2 = dx[1] - dy[0]
            square = dx[0] * dx[0] + dy[1] * dy[1] + dz[2] * dz[2]
            square = square + 2.0 * (dy[0] * dx[1] + dz[0] * dx[2] + dz[1] * dy[2])
            spin = w0 * w0 + w1 * w1 + w2 * w2
            seen = count > odd * (slab - 1 - 2 * q) + q
            passed, values, strength = shade(square, spin, seen, pairs, total_depth)
            weight = (1.0 - passed) * (strength * (1.0 / UNIT))
            layers.append([weight * value for value in values] + [passed])
        first = [jnp.where(front, a, b) for a, b in zip(layers[0], layers[2])]
        last = [jnp.where(front, b, a) for a, b in zip(layers[0], layers[2])]
        clear = first[3] * layers[1][3]
        rest = part[3, rows, :]
        outer_clear = clear * last[3]
        image = []
        for k in range(3):
            edge = first[k] + first[3] * layers[1][k] + clear * last[k]
            inner = part[k, rows, :]
            image.append(jnp.where(front, edge + outer_clear * inner, inner + rest * edge))
        return image + [1.0 - outer_clear * rest]

    owner = odd if own else 1 - odd
    starts = sorted({min(w, max(share - SUB, 0)) for w in range(0, share, SUB)})
    height = min(share, SUB)
    for s in range(chips):
        chip = owner_chip(me // 2, s, chips)
        for w in starts:
            row = (2 * chip + owner) * share + w
            image = window(pl.ds(row, SUB))
            for k in range(4):
                out[s, k, pl.ds(w, height), :] = image[k][:height]


def over(front, back):
    return front + (1.0 - front[..., 3:, :, :]) * back


def gather_rays(mine, theirs):
    chips = mine.shape[0]
    devices = 2 * chips
    me = lax.axis_index("depth")
    odd = lax.rem(me, 2) == 1
    theirs = lax.ppermute(theirs, "depth", [(i, i + 1 - 2 * (i % 2)) for i in range(devices)])
    both = over(jnp.where(odd, theirs, mine), jnp.where(odd, mine, theirs))
    chip = me // 2
    if chips in (2, 4):
        step, source = (2, 1, 3), lambda k: chip ^ k
        rings = {k: [(i, i ^ (2 * k)) for i in range(devices)] for k in range(1, chips)}
    else:
        step, source = range(1, chips), lambda k: lax.rem(chip - k + chips, chips)
        rings = {k: [(i, (i + 2 * k) % devices) for i in range(devices)] for k in range(1, chips)}
    order = [0] + [k for k in step if k < chips]
    got = [both[0]] + [lax.ppermute(both[k], "depth", rings[k]) for k in order[1:]]
    chip_of = [source(k) for k in order]
    weights, image = [], 0.0
    for n, layer in enumerate(got):
        clear = 1.0 - layer[3:]
        weights = [
            w * jnp.where(chip_of[n] < chip_of[m], clear, 1.0) for m, w in enumerate(weights)
        ]
        own = jnp.ones_like(clear)
        for m in range(n):
            own = own * jnp.where(chip_of[m] < chip_of[n], 1.0 - got[m][3:], 1.0)
        weights.append(own)
    return sum(w * layer for w, layer in zip(weights, got))


def vmem(count):
    return [pl.BlockSpec(memory_space=pltpu.VMEM)] * count


def held(*dims):
    return pltpu.VMEM(dims, F32)


def in_vmem(x):
    return pltpu.with_memory_space_constraint(x, pltpu.VMEM)


def per_device(velocity, metric, colour_map, counts):
    _, slab, ny, cx = velocity.shape
    devices = lax.axis_size("depth")
    tiles = lax.axis_size("tile")
    total_depth = slab * devices
    scalars = pl.BlockSpec(memory_space=pltpu.SMEM)

    def limit(size):
        return pltpu.CompilerParams(vmem_limit_bytes=size * MIB)

    hbm = pl.BlockSpec(memory_space=pltpu.HBM)
    share = ny // devices
    spare = SUB if share < SUB else 0
    padded = (3, slab + 2 * REACH, ny + 2 * SUB, cx)
    columns = (3, ny // 2, cx)
    up = [(i, (i + 1) % devices) for i in range(devices)]
    down = [(i, (i - 1) % devices) for i in range(devices)]
    whole = pltpu.with_memory_space_constraint(velocity, pltpu.HBM)
    near, far = pl.pallas_call(
        ends_kernel,
        out_shape=(held(3, REACH, ny, cx), held(3, REACH, ny + spare, cx)),
        in_specs=[hbm],
        out_specs=tuple(vmem(2)),
        scratch_shapes=[pltpu.SemaphoreType.DMA((2,))],
        compiler_params=limit(4),
        name="ends",
    )(whole)
    near = lax.ppermute(near, "depth", [(down if i % 2 else up)[i] for i in range(devices)])
    far = lax.ppermute(far, "depth", [(up if i % 2 else down)[i] for i in range(devices)])

    ext, to_right, to_left = pl.pallas_call(
        edges_kernel,
        out_shape=(held(*padded), held(*columns), held(*columns)),
        in_specs=vmem(1),
        out_specs=tuple(vmem(3)),
        scratch_shapes=[pltpu.SemaphoreType.DMA((1,))],
        compiler_params=limit(4),
        name="edges",
    )(velocity)
    from_left = lax.ppermute(to_right, "tile", [(i, (i + 1) % tiles) for i in range(tiles)])
    from_right = lax.ppermute(to_left, "tile", [(i, (i - 1) % tiles) for i in range(tiles)])

    stream, span, outline = pl.pallas_call(
        slopes_kernel,
        out_shape=(
            held(3, slab, ny, cx),
            held(4, slab, ny, cx),
            held(6, REACH, ny + spare, cx),
        ),
        in_specs=vmem(2) + [scalars],
        out_specs=tuple(vmem(3)),
        scratch_shapes=[pltpu.VMEM((2 * cx, cx), BF16)],
        compiler_params=limit(4),
        name="slopes",
    )(in_vmem(ext), in_vmem(near), metric)

    part, stream = pl.pallas_call(
        functools.partial(inner_kernel, total_depth),
        out_shape=(held(4, ny + spare, cx), held(3, REACH, ny + spare, cx)),
        in_specs=vmem(6),
        out_specs=tuple(vmem(2)),
        scratch_shapes=[
            pltpu.VMEM((3 * ny, slab * cx), F32),
            pltpu.VMEM((3 * ny, 2 * cx), BF16),
            pltpu.VMEM((2 * cx, cx), F32),
        ],
        compiler_params=limit(8),
        name="inner",
    )(*map(in_vmem, (stream, span, from_left, from_right, counts, colour_map)))

    tall = jnp.pad(counts, ((0, spare), (0, 0))) if spare else counts
    rest = tuple(map(in_vmem, (far, outline, stream, part, tall, colour_map)))

    def outer(own, name):
        return pl.pallas_call(
            functools.partial(outer_kernel, total_depth, own),
            out_shape=held(devices // 2, 4, share, cx),
            in_specs=vmem(6),
            out_specs=vmem(1)[0],
            compiler_params=limit(4),
            name=name,
        )(*rest)

    theirs = outer(False, "theirs")
    return gather_rays(outer(True, "mine"), theirs)


def solution(mesh):
    in_specs = (P(None, "depth", None, "tile"), P(), P(), P(None, "tile"))
    out_specs = P(None, "depth", "tile")
    return jax.shard_map(
        per_device, mesh=mesh, in_specs=in_specs, out_specs=out_specs, check_vma=False
    )
```
